128 devices in a mesh: row: 8 (over y, core), col: 16 (over x, z).
Axes of the slice: x: 4, y: 4, z: 4, core: 2. Of those that a mesh axis runs over, the one named last changes fastest.
Arguments:
- grad: bfloat16 [8192, 4096], P('row', 'col'), may hold values from -6 to 6
- basis_left: bfloat16 [8192, 8192], P('row', 'col'), may hold values from -0.0625 to 0.0625
- basis_right: bfloat16 [4096, 4096], P('row', 'col'), may hold values from -0.09375 to 0.09375
- first_moment: float32 [8192, 4096], P('col', 'row'), may hold values from -6 to 6
- second_moment: float32 [8192, 4096], P('col', 'row'), may hold values from 0.25 to 4
Outputs:
- update: bfloat16 [8192, 4096], P('row', 'col')
- first_new: float32 [8192, 4096], P('col', 'row')
- second_new: float32 [8192, 4096], P('col', 'row')
The draws below stay inside these ranges and needn't reach their ends.
All inputs are finite; a program needn't handle non-finite values.
Results may differ from the reference program's by a relative error of at most 0.029.
Values may be sent and summed in bfloat16 or wider, within the bound.
A program may use at most 64 MiB of HBM per device.

```python
import math
import jax
import jax.numpy as jnp
from jax import lax

M = 8192
NB = 4096
N_ROW = 8
N_COL = 16


def block_levels(stream_key, shape, cuts, low, largest):
    factor_of = 1.0
    for dim, shards_of in cuts:
        draws = jax.random.uniform(jax.random.fold_in(jax.random.fold_in(stream_key, 6), dim), (shards_of,), jnp.float32, low / len(cuts), largest / len(cuts))
        factor_of = factor_of * jnp.repeat(jnp.exp(draws), shape[dim] // shards_of).reshape((-1,) + (1,) * (len(shape) - 1 - dim))
    return factor_of


def scatter_about(stream_key, shape, spread, reach, shards=(), kind=jnp.bfloat16):
    loudness = block_levels(stream_key, shape, shards, -0.22, 0.18) if shards else 1.0
    array = jax.random.normal(stream_key, shape, jnp.float32) * spread * loudness
    return jnp.minimum(jnp.maximum(array, -reach), reach).astype(kind)


def setup_inputs(seed: int = 0) -> dict:
    key_list = jax.random.split(jax.random.key(seed), 6)
    grad = scatter_about(key_list[0], (M, NB), 1.0, 6.0, ((0, 8), (1, 16)))
    basis_left = scatter_about(key_list[1], (M, M), M ** -0.5, 0.0625, ((0, 8), (1, 16)))
    basis_right = scatter_about(key_list[2], (NB, NB), NB ** -0.5, 0.09375, ((0, 8), (1, 16)))
    first_moment = scatter_about(key_list[3], (M, NB), 1.0, 6.0, ((0, 16), (1, 8)), jnp.float32)
    second_moment = jnp.clip(jnp.exp(math.log(4.0) - 2.7725887 * jax.random.uniform(key_list[4], (M, NB), jnp.float32) ** block_levels(key_list[4], (M, NB), ((0, 16), (1, 8)), -0.2, 0.2)), 0.25, 4.0)
    return dict(grad=grad, basis_left=basis_left, basis_right=basis_right, first_moment=first_moment, second_moment=second_moment)


def rounded_sum(pairs):
    total = None
    for left_part, right_part in pairs:
        product = jnp.dot(left_part, right_part, preferred_element_type=jnp.float32)
        product = lax.optimization_barrier(product.astype(jnp.bfloat16)).astype(jnp.float32)
        total = product if total is None else total + product
    return total

def reference(grad, basis_left, basis_right, first_moment, second_moment):
    row_block = M // N_ROW
    left_rotated = rounded_sum([(basis_left[b * row_block:(b + 1) * row_block, :].T, grad[b * row_block:(b + 1) * row_block, :]) for b in range(N_ROW)]).astype(jnp.bfloat16)
    col_block = NB // N_ROW
    rotated = rounded_sum([(left_rotated[:, b * col_block:(b + 1) * col_block], basis_right[b * col_block:(b + 1) * col_block, :]) for b in range(N_ROW)])
    first_new = 0.9 * first_moment + 0.1 * rotated
    second_new = 0.95 * second_moment + 0.05 * rotated * rotated
    direction = (first_new / (jnp.sqrt(second_new) + 1e-08)).astype(jnp.bfloat16)
    inner_block = M // N_COL
    back_left = rounded_sum([(basis_left[:, b * inner_block:(b + 1) * inner_block], direction[b * inner_block:(b + 1) * inner_block, :]) for b in range(N_COL)]).astype(jnp.bfloat16)
    last_block = NB // N_COL
    update = rounded_sum([(back_left[:, b * last_block:(b + 1) * last_block], basis_right[:, b * last_block:(b + 1) * last_block].T) for b in range(N_COL)]).astype(jnp.bfloat16)
    return (update, first_new, second_new)
```

```python
import functools

import jax
import jax.numpy as jnp
from jax import lax
from jax.experimental import pallas as pl
from jax.experimental.pallas import tpu as pltpu
from jax.sharding import PartitionSpec as P

MESH = pl.DeviceIdType.MESH
BF = jnp.bfloat16
F32 = jnp.float32
NK = 2
NM = 2
KC = 1024 // NK
MC = 1024 // NM
MT = MC // 4
OPS = ("g", "trs", "tag", "rrs", "dag", "brs", "bag", "urs")


def wrap(v):
    return lax.rem(v + 8, 4)


def kernel(
    g_ref, l_ref, r_ref, fm_ref, sm_ref,
    u_ref, fn_ref, sn_ref,
    gx, rb, tp, t_own, tx, lh, pp, qq, rot_own, rot_home, d_home, d_own, dall, blp, bl_own, blz, up,
    t_comb, t_fin, r_comb, r_fin, b_comb, b_fin, u_comb, u_fin,
    ring_s, ring_r, l_s, l_r, ra_s, ra_r, r1_s, r1_r, rsib_s, rsib_r, psib_s, psib_r,
    fwd_s, fwd_r, back_s, back_r, dsib_s, dsib_r,
):
    row, col = lax.axis_index("row"), lax.axis_index("col")
    y, c, x, z = row // 2, lax.rem(row, 2), col // 4, lax.rem(col, 4)
    other = 1 - c

    def dev(x, y, z, c):
        return (y * 2 + c, x * 4 + z)

    sib = dev(x, y, z, other)
    ring = {
        "x": (x, dev(wrap(x + 1), y, z, c), dev(wrap(x - 1), y, z, c)),
        "y": (y, dev(x, wrap(y + 1), z, c), dev(x, wrap(y - 1), z, c)),
        "z": (z, dev(x, y, wrap(z + 1), c), dev(x, y, wrap(z - 1), c)),
    }

    barrier = pltpu.get_barrier_semaphore()
    partners = [ring["x"][1], ring["x"][2], ring["y"][1], ring["y"][2], sib]
    for d in (1, 2, 3):
        partners += [dev(x, y, wrap(z + d), c), dev(x, y, wrap(z + d), other)]
    for partner in partners:
        pl.semaphore_signal(barrier, inc=1, device_id=partner, device_id_type=MESH)
    pl.semaphore_wait(barrier, len(partners))

    sent = []

    def send(src, dst, ssem, rsem, device):
        copy = pltpu.make_async_remote_copy(
            src_ref=src, dst_ref=dst, send_sem=ssem, recv_sem=rsem, device_id=device, device_id_type=MESH
        )
        copy.start()
        sent.append((None, copy))

    def arrived(dst, ssem, rsem):
        pltpu.make_async_remote_copy(
            src_ref=dst, dst_ref=dst, send_sem=ssem, recv_sem=rsem, device_id=sib, device_id_type=MESH
        ).wait_recv()

    def send_or_keep(mine, src, dst, ssem, rsem, device):
        copy = pltpu.make_async_remote_copy(
            src_ref=src, dst_ref=dst, send_sem=ssem, recv_sem=rsem, device_id=device, device_id_type=MESH
        )

        @pl.when(jnp.logical_not(mine))
        def _():
            copy.start()

        @pl.when(mine)
        def _():
            dst[...] = src[...]

        sent.append((mine, copy))

    def arrived_or_kept(mine, dst, ssem, rsem):
        @pl.when(jnp.logical_not(mine))
        def _():
            arrived(dst, ssem, rsem)

    class Ring:
        def __init__(self, axis, ssem, rsem, half):
            self.pos, self.right_dev, self.left_dev = ring[axis]
            self.right, self.left, self.opp = wrap(self.pos + 1), wrap(self.pos - 1), wrap(self.pos + 2)
            self.ssem, self.rsem, self.half = ssem, rsem, half

        def go(self, j, n, src, dst):
            send(src, dst, self.ssem(j, n), self.rsem(j, n), self.right_dev if n < 3 else self.left_dev)

        def wait(self, j, n, dst):
            arrived(dst, self.ssem(j, n), self.rsem(j, n))

        def rows(self, j, h):
            return pl.ds((2 * j + h) * self.half, self.half)

    class Gather(Ring):
        def __init__(self, axis, ssem, rsem, half, src, dst):
            super().__init__(axis, ssem, rsem, half)
            self.src, self.dst = src, dst

        def start(self, j, keep=True):
            a, b = self.rows(j, 0), self.rows(j, 1)
            self.go(j, 0, self.src(a), self.dst(self.pos, a))
            self.go(j, 3, self.src(b), self.dst(self.pos, b))
            self.go(j, 1, self.src(b), self.dst(self.pos, b))
            self.go(j, 4, self.src(a), self.dst(self.pos, a))
            if keep:
                for r in (a, b):
                    self.dst(self.pos, r)[...] = self.src(r)[...]

        def mid(self, j):
            a, b = self.rows(j, 0), self.rows(j, 1)
            self.wait(j, 0, self.dst(self.left, a))
            self.go(j, 2, self.dst(self.left, a), self.dst(self.left, a))
            self.wait(j, 3, self.dst(self.right, b))
            self.go(j, 5, self.dst(self.right, b), self.dst(self.right, b))

        def end(self, j):
            a, b = self.rows(j, 0), self.rows(j, 1)
            self.wait(j, 1, self.dst(self.left, b))
            self.wait(j, 4, self.dst(self.right, a))
            self.wait(j, 2, self.dst(self.opp, a))
            self.wait(j, 5, self.dst(self.opp, b))

    class Scatter(Ring):
        def __init__(self, axis, ssem, rsem, half, piece, comb, fin, out):
            super().__init__(axis, ssem, rsem, half)
            self.piece, self.comb, self.fin, self.out = piece, comb, fin, out

        def start(self, j):
            a, b = self.rows(j, 0), self.rows(j, 1)
            self.go(j, 0, self.piece(self.opp, a), self.comb.at[j, 0])
            self.go(j, 3, self.piece(self.opp, b), self.comb.at[j, 1])
            self.go(j, 1, self.piece(self.right, b), self.fin.at[j, 0, 1])
            self.go(j, 4, self.piece(self.left, a), self.fin.at[j, 1, 0])

        def mid(self, j):
            a, b = self.rows(j, 0), self.rows(j, 1)
            for n, side, r, h in ((0, self.right, a, 0), (3, self.left, b, 1)):
                self.wait(j, n, self.comb.at[j, h])
                ref = self.piece(side, r)
                ref[...] = (ref[...].astype(F32) + self.comb[j, h].astype(F32)).astype(BF)
                self.go(j, n + 2, ref, self.fin.at[j, h, h])

        def end(self, j):
            for h, first, second in ((0, 4, 2), (1, 1, 5)):
                r = self.rows(j, h)
                self.wait(j, first, self.fin.at[j, 1 - h, h])
                self.wait(j, second, self.fin.at[j, h, h])
                total = self.piece(self.pos, r)[...].astype(F32)
                total = total + self.fin[j, 0, h].astype(F32) + self.fin[j, 1, h].astype(F32)
                self.out(r)[...] = total.astype(BF)

    def ring_sems(name):
        i = OPS.index(name)
        return (lambda j, n: ring_s.at[i, j, n]), (lambda j, n: ring_r.at[i, j, n])

    def columns(ref, n, width=256):
        return lambda t, r: ref.at[r, pl.ds(pl.multiple_of(t * width, width), width)]

    def pieces(ref):
        return lambda t, r: ref.at[t, r]

    kh, mh = KC // 2, MC // 2
    g_ag = Gather("x", *ring_sems("g"), kh, lambda r: g_ref.at[r], columns(gx, 4))
    t_rs = Scatter("z", *ring_sems("trs"), kh, pieces(tp), t_comb, t_fin, lambda r: t_own.at[r])
    t_ag = Gather("x", *ring_sems("tag"), kh, lambda r: t_own.at[r], pieces(tx))
    r_rs = Scatter("y", *ring_sems("rrs"), mh, lambda t, r: pp.at[c, t, r], r_comb, r_fin, lambda r: rot_own.at[r])
    d_ag = Gather("y", *ring_sems("dag"), mh, lambda r: d_own.at[r], lambda t, r: dall.at[c, t, r])
    b_rs = Scatter("x", *ring_sems("brs"), kh, pieces(blp), b_comb, b_fin, lambda r: bl_own.at[r])
    b_ag = Gather("z", *ring_sems("bag"), kh, lambda r: bl_own.at[r], columns(blz, 4))
    u_rs = Scatter("x", *ring_sems("urs"), kh, pieces(up), u_comb, u_fin, lambda r: u_ref.at[r])

    def l_unit(h, j):
        i = h * NM + j
        return Gather(
            "z",
            lambda _, n: l_s.at[i, n],
            lambda _, n: l_r.at[i, n],
            512,
            lambda r: l_ref.at[r, pl.ds(h * 256 + j * MT, MT)],
            lambda t, r: lh.at[h, r, pl.ds(pl.multiple_of(j * MC + t * MT, MT), MT)],
        )

    l_units = [l_unit(h, j) for j in range(NM) for h in range(2)]

    def rb_block(t, cc):
        return rb.at[pl.ds(pl.multiple_of(t * 256 + cc * 128, 128), 128)]

    def rb_rows(t, r):
        return rb.at[pl.ds(pl.multiple_of(t * 256 + c * 128 + r.start, 64), r.size)]

    r_ag = Gather("y", lambda _, n: ra_s.at[n], lambda _, n: ra_r.at[n], 64, lambda r: rb_rows(y, r), rb_rows)

    def rb_tile(cc, zz):
        return rb.at[
            pl.ds(pl.multiple_of(y * 256 + cc * 128, 128), 128), pl.ds(pl.multiple_of(zz * 256, 256), 256)
        ]

    for sl in range(2):
        for cc in range(2):
            mine = jnp.logical_and(2 * c + sl == z, c == cc)
            send_or_keep(
                mine, r_ref.at[pl.ds(sl * 256 + cc * 128, 128)], rb_tile(cc, z),
                r1_s.at[sl, cc], r1_r.at[z], dev(x, y, 2 * c + sl, cc),
            )
    for j in range(NK):
        g_ag.start(j)
    for unit in l_units:
        unit.start(0)
    for zz in range(4):
        mine = jnp.logical_and(zz == z, z // 2 == c)
        arrived_or_kept(mine, rb_tile(c, zz), r1_s.at[0, 0], r1_r.at[zz])
    r_ag.start(0, keep=False)

    def sib_block(t, n):
        send(rb_block(t, c), rb_block(t, c), rsib_s.at[n], rsib_r.at[n], sib)

    sib_block(y, 0)
    g_ag.mid(0)
    r_ag.mid(0)
    for j in range(1, NK):
        g_ag.mid(j)
    r_ag.end(0)
    for n, t in enumerate((r_ag.left, r_ag.right, r_ag.opp)):
        sib_block(t, n + 1)
    for n, t in enumerate((y, r_ag.left, r_ag.right, r_ag.opp)):
        arrived(rb_block(t, other), rsib_s.at[n], rsib_r.at[n])

    def rotate_right(j):
        rows = pl.ds(j * KC, KC)

        def body(b, _):
            right = rb[:, pl.ds(pl.multiple_of(b * 256, 256), 256)]
            tp[b, rows] = jnp.dot(gx[rows], right, preferred_element_type=F32).astype(BF)
            return 0

        lax.fori_loop(0, 4, body, 0)

    for j in range(NK):
        g_ag.end(j)
        rotate_right(j)
        t_rs.start(j)
    for j in range(NK):
        t_rs.mid(j)
    for unit in l_units:
        unit.mid(0)
    for j in range(NK):
        t_rs.end(j)
        t_ag.start(j)
    for j in range(NK):
        t_ag.mid(j)
    for unit in l_units:
        unit.end(0)
    for j in range(NK):
        t_ag.end(j)

    def rotate_left(h, j):
        rows = pl.ds(j * MC, MC)

        def body(a, _):
            pp[h, a, rows] = lax.dot_general(
                lh[h, :, rows], tx[a], (((0,), (0,)), ((), ())), preferred_element_type=F32
            ).astype(BF)
            return 0

        lax.fori_loop(0, 4, body, 0)

    for j in range(NM):
        rows = pl.ds(j * MC, MC)
        rotate_left(other, j)
        for a in range(4):
            send(pp.at[other, a, rows], qq.at[a, rows], psib_s.at[j, a], psib_r.at[j, a], sib)
        rotate_left(c, j)
    for j in range(NM):
        rows = pl.ds(j * MC, MC)
        for a in range(4):
            arrived(qq.at[a, rows], psib_s.at[j, a], psib_r.at[j, a])
            pp[c, a, rows] = (pp[c, a, rows].astype(F32) + qq[a, rows].astype(F32)).astype(BF)
        r_rs.start(j)
    for j in range(NM):
        r_rs.mid(j)

    def home_tile(ref, cc, s, j):
        return ref.at[
            pl.ds(pl.multiple_of(cc * 256 + j * MT, MT), MT), pl.ds(pl.multiple_of(s * 256, 256), 256)
        ]

    def own_tile(ref, zz, j):
        return ref.at[pl.ds(pl.multiple_of(j * MC + zz * MT, MT), MT)]

    for j in range(NM):
        r_rs.end(j)
        for d in range(4):
            zz = wrap(z + d)
            place = (own_tile(rot_own, zz, j), home_tile(rot_home, c, lax.rem(z, 2), j),
                     fwd_s.at[j, d], fwd_r.at[j, lax.rem(z, 2) * 2 + c], dev(x, y, zz, z // 2))
            if d:
                send(*place)
            else:
                send_or_keep(z // 2 == c, *place)
    for j in range(NM):
        for s in range(2):
            for cc in range(2):
                mine = jnp.logical_and(2 * c + s == z, c == cc)
                arrived_or_kept(mine, home_tile(rot_home, cc, s, j), fwd_s.at[j, 0], fwd_r.at[j, s * 2 + cc])
        for h in range(2):
            rows = pl.ds(h * 256 + j * MT, MT)
            rotated = rot_home[rows].astype(F32)
            first = 0.9 * fm_ref[rows] + 0.1 * rotated
            second = 0.95 * sm_ref[rows] + 0.05 * rotated * rotated
            fn_ref[rows] = first
            sn_ref[rows] = second
            d_home[rows] = (first / (jnp.sqrt(second) + 1e-08)).astype(BF)
        for h in range(2):
            for s in range(2):
                mine = jnp.logical_and(2 * c + s == z, c == h)
                send_or_keep(
                    mine, home_tile(d_home, h, s, j), own_tile(d_own, z, j),
                    back_s.at[j, h, s], back_r.at[j, z], dev(x, y, 2 * c + s, h),
                )
    for j in range(NM):
        for zz in range(4):
            mine = jnp.logical_and(zz == z, z // 2 == c)
            arrived_or_kept(mine, own_tile(d_own, zz, j), back_s.at[j, 0, 0], back_r.at[j, zz])
        d_ag.start(j)

    def d_block(t, j, cc):
        return dall.at[cc, t, pl.ds(j * MC, MC)]

    order = (y, d_ag.left, d_ag.right, d_ag.opp)
    for j in range(NM):
        send(d_block(y, j, c), d_block(y, j, c), dsib_s.at[j, 0], dsib_r.at[j, 0], sib)
        d_ag.mid(j)
    for j in range(NM):
        d_ag.end(j)
        for n in (1, 2, 3):
            send(d_block(order[n], j, c), d_block(order[n], j, c), dsib_s.at[j, n], dsib_r.at[j, n], sib)
    for j in range(NM):
        for n in range(4):
            arrived(d_block(order[n], j, other), dsib_s.at[j, n], dsib_r.at[j, n])

    def rotate_back_left(j):
        rows = pl.ds(j * KC, KC)

        def body(a, _):
            total = jnp.dot(lh[0, rows], dall[0, a], preferred_element_type=F32)
            total = total + jnp.dot(lh[1, rows], dall[1, a], preferred_element_type=F32)
            blp[a, rows] = total.astype(BF)
            return 0

        lax.fori_loop(0, 4, body, 0)

    def rotate_back_right(j):
        rows = pl.ds(j * KC, KC)

        def body(t, _):
            right = rb[pl.ds(pl.multiple_of(t * 256, 256), 256)]
            up[t, rows] = lax.dot_general(
                blz[rows], right, (((1,), (1,)), ((), ())), preferred_element_type=F32
            ).astype(BF)
            return 0

        lax.fori_loop(0, 4, body, 0)

    for j in range(NK):
        rotate_back_left(j)
        b_rs.start(j)
    for j in range(NK):
        b_rs.mid(j)
    for j in range(NK):
        b_rs.end(j)
        b_ag.start(j)
    for j in range(NK):
        b_ag.mid(j)
    for j in range(NK):
        b_ag.end(j)
        rotate_back_right(j)
        u_rs.start(j)
    for j in range(NK):
        u_rs.mid(j)
    for j in range(NK):
        u_rs.end(j)

    for mine, copy in sent:
        if mine is None:
            copy.wait_send()
        else:
            @pl.when(jnp.logical_not(mine))
            def _(copy=copy):
                copy.wait_send()


def per_device(grad, basis_left, basis_right, first_moment, second_moment):
    dma = pltpu.SemaphoreType.DMA
    kh, mh = KC // 2, MC // 2

    def scatter_buffers(chunks, half):
        return [pltpu.VMEM((chunks, 2, half, 256), BF), pltpu.VMEM((chunks, 2, 2, half, 256), BF)]

    scratch = [
        pltpu.VMEM((1024, 1024), BF),
        pltpu.VMEM((1024, 1024), BF),
        pltpu.VMEM((4, 1024, 256), BF),
        pltpu.VMEM((1024, 256), BF),
        pltpu.VMEM((4, 1024, 256), BF),
        pltpu.VMEM((2, 1024, 1024), BF),
        pltpu.VMEM((2, 4, 1024, 256), BF),
        pltpu.VMEM((4, 1024, 256), BF),
        pltpu.VMEM((1024, 256), BF),
        pltpu.VMEM((512, 512), BF),
        pltpu.VMEM((512, 512), BF),
        pltpu.VMEM((1024, 256), BF),
        pltpu.VMEM((2, 4, 1024, 256), BF),
        pltpu.VMEM((4, 1024, 256), BF),
        pltpu.VMEM((1024, 256), BF),
        pltpu.VMEM((1024, 1024), BF),
        pltpu.VMEM((4, 1024, 256), BF),
    ]
    scratch += scatter_buffers(NK, kh) + scatter_buffers(NM, mh) + scatter_buffers(NK, kh) + scatter_buffers(NK, kh)
    most = max(NK, NM)
    for out, back in (
        ((len(OPS), most, 6), (len(OPS), most, 6)), ((2 * NM, 6), (2 * NM, 6)), ((6,), (6,)), ((2, 2), (4,)),
        ((4,), (4,)), ((NM, 4), (NM, 4)), ((NM, 4), (NM, 4)), ((NM, 2, 2), (NM, 4)), ((NM, 4), (NM, 4)),
    ):
        scratch += [dma(out), dma(back)]
    vmem = pl.BlockSpec(memory_space=pltpu.VMEM)
    return pl.pallas_call(
        kernel,
        out_shape=(
            jax.ShapeDtypeStruct((1024, 256), BF),
            jax.ShapeDtypeStruct((512, 512), F32),
            jax.ShapeDtypeStruct((512, 512), F32),
        ),
        in_specs=[vmem] * 5,
        out_specs=[vmem] * 3,
        scratch_shapes=scratch,
        compiler_params=pltpu.CompilerParams(
            collective_id=0, has_side_effects=True, vmem_limit_bytes=60 * 1024 * 1024
        ),
        cost_estimate=pl.CostEstimate(flops=12884901888, bytes_accessed=6553600, transcendentals=262144),
    )(grad, basis_left, basis_right, first_moment, second_moment)


def solution(mesh):
    in_specs = (P("row", "col"), P("row", "col"), P("row", "col"), P("col", "row"), P("col", "row"))
    out_specs = (P("row", "col"), P("col", "row"), P("col", "row"))
    return jax.shard_map(
        per_device, mesh=mesh, in_specs=in_specs, out_specs=out_specs, check_vma=False
    )
```

```python
import functools

import jax
import jax.numpy as jnp
from jax import lax
from jax.experimental import pallas as pl
from jax.experimental.pallas import tpu as pltpu
from jax.sharding import PartitionSpec as P

MESH = pl.DeviceIdType.MESH
BF = jnp.bfloat16
F32 = jnp.float32
NK = 4
KC = 1024 // NK
NQ = 4
OPS = ("g", "trs", "tag", "rrs", "dag", "brs", "bag", "urs")


def wrap(v):
    return lax.rem(v + 8, 4)


def kernel(
    g_ref, l_ref, r_ref, fm_ref, sm_ref,
    u_ref, fn_ref, sn_ref,
    gx, rb, tp, tx, lh, pp, qq, rot_own, rot_home, d_home, dall, blp, blz, up, u_out, fm, sm,
    t_comb, t_fin, r_comb, r_fin, b_comb, b_fin, u_comb, u_fin,
    ring_s, ring_r, l_s, l_r, ra_s, ra_r, r1_s, r1_r, rsib_s, rsib_r, psib_s, psib_r,
    fwd_s, fwd_r, back_s, back_r, dsib_s, dsib_r, near,
):
    row, col = lax.axis_index("row"), lax.axis_index("col")
    y, c, x, z = row // 2, lax.rem(row, 2), col // 4, lax.rem(col, 4)
    other = 1 - c

    def dev(x, y, z, c):
        return (y * 2 + c, x * 4 + z)

    sib = dev(x, y, z, other)
    ring = {
        "x": (x, dev(wrap(x + 1), y, z, c), dev(wrap(x - 1), y, z, c)),
        "y": (y, dev(x, wrap(y + 1), z, c), dev(x, wrap(y - 1), z, c)),
        "z": (z, dev(x, y, wrap(z + 1), c), dev(x, y, wrap(z - 1), c)),
    }

    barrier = pltpu.get_barrier_semaphore()
    partners = [ring["x"][1], ring["x"][2], ring["y"][1], ring["y"][2], sib]
    for d in (1, 2, 3):
        partners += [dev(x, y, wrap(z + d), c), dev(x, y, wrap(z + d), other)]
    for partner in partners:
        pl.semaphore_signal(barrier, inc=1, device_id=partner, device_id_type=MESH)
    pl.semaphore_wait(barrier, len(partners))

    sent = []

    def send(src, dst, ssem, rsem, device):
        copy = pltpu.make_async_remote_copy(
            src_ref=src, dst_ref=dst, send_sem=ssem, recv_sem=rsem, device_id=device, device_id_type=MESH
        )
        copy.start()
        sent.append((None, copy))

    def local(src, dst, n):
        copy = pltpu.make_async_copy(src, dst, near.at[n])
        copy.start()
        return copy

    def arrived(dst, ssem, rsem):
        pltpu.make_async_remote_copy(
            src_ref=dst, dst_ref=dst, send_sem=ssem, recv_sem=rsem, device_id=sib, device_id_type=MESH
        ).wait_recv()

    def send_or_keep(mine, src, dst, ssem, rsem, device, by_copy=None):
        copy = pltpu.make_async_remote_copy(
            src_ref=src, dst_ref=dst, send_sem=ssem, recv_sem=rsem, device_id=device, device_id_type=MESH
        )

        @pl.when(jnp.logical_not(mine))
        def _():
            copy.start()

        @pl.when(mine)
        def _():
            if by_copy is None:
                dst[...] = src[...]
            else:
                kept = pltpu.make_async_copy(src, dst, by_copy)
                kept.start()
                kept.wait()

        sent.append((mine, copy))

    def arrived_or_kept(mine, dst, ssem, rsem):
        @pl.when(jnp.logical_not(mine))
        def _():
            arrived(dst, ssem, rsem)

    class Ring:
        def __init__(self, axis, ssem, rsem, half):
            self.pos, self.right_dev, self.left_dev = ring[axis]
            self.right, self.left, self.opp = wrap(self.pos + 1), wrap(self.pos - 1), wrap(self.pos + 2)
            self.ssem, self.rsem, self.half = ssem, rsem, half

        def go(self, j, n, src, dst):
            send(src, dst, self.ssem(j, n), self.rsem(j, n), self.right_dev if n < 3 else self.left_dev)

        def wait(self, j, n, dst):
            arrived(dst, self.ssem(j, n), self.rsem(j, n))

        def rows(self, j, h):
            if self.half is None:
                return (j // 2, pl.ds(2 * h, 2), j % 2)
            return (pl.ds((2 * j + h) * self.half, self.half),)

    class Gather(Ring):
        def __init__(self, axis, ssem, rsem, half, src, dst):
            super().__init__(axis, ssem, rsem, half)
            self.src, self.dst = src, dst

        def start(self, j):
            a, b = self.rows(j, 0), self.rows(j, 1)
            self.go(j, 0, self.src(a), self.dst(self.pos, a))
            self.go(j, 3, self.src(b), self.dst(self.pos, b))
            self.go(j, 1, self.src(b), self.dst(self.pos, b))
            self.go(j, 4, self.src(a), self.dst(self.pos, a))

        def mid(self, j):
            a, b = self.rows(j, 0), self.rows(j, 1)
            self.wait(j, 0, self.dst(self.left, a))
            self.go(j, 2, self.dst(self.left, a), self.dst(self.left, a))
            self.wait(j, 3, self.dst(self.right, b))
            self.go(j, 5, self.dst(self.right, b), self.dst(self.right, b))

        def end(self, j):
            a, b = self.rows(j, 0), self.rows(j, 1)
            self.wait(j, 1, self.dst(self.left, b))
            self.wait(j, 4, self.dst(self.right, a))
            self.wait(j, 2, self.dst(self.opp, a))
            self.wait(j, 5, self.dst(self.opp, b))

    class Scatter(Ring):
        def __init__(self, axis, ssem, rsem, half, piece, comb, fin, out):
            super().__init__(axis, ssem, rsem, half)
            self.piece, self.comb, self.fin, self.out = piece, comb, fin, out

        def start(self, j):
            a, b = self.rows(j, 0), self.rows(j, 1)
            self.go(j, 0, self.piece(self.opp, a), self.comb.at[j, 0])
            self.go(j, 3, self.piece(self.opp, b), self.comb.at[j, 1])
            self.go(j, 1, self.piece(self.right, b), self.fin.at[j, 0, 1])
            self.go(j, 4, self.piece(self.left, a), self.fin.at[j, 1, 0])

        def mid(self, j):
            a, b = self.rows(j, 0), self.rows(j, 1)
            for n, side, r, h in ((0, self.right, a, 0), (3, self.left, b, 1)):
                self.wait(j, n, self.comb.at[j, h])
                ref = self.piece(side, r)
                ref[...] = (ref[...].astype(F32) + self.comb[j, h].astype(F32)).astype(BF)
                self.go(j, n + 2, ref, self.fin.at[j, h, h])

        def end(self, j):
            for h, first, second in ((0, 4, 2), (1, 1, 5)):
                r = self.rows(j, h)
                self.wait(j, first, self.fin.at[j, 1 - h, h])
                self.wait(j, second, self.fin.at[j, h, h])
                total = self.piece(self.pos, r)[...].astype(F32)
                total = total + self.fin[j, 0, h].astype(F32) + self.fin[j, 1, h].astype(F32)
                self.out(r)[...] = total.astype(BF)

    def ring_sems(name):
        i = OPS.index(name)
        return (lambda j, n: ring_s.at[i, j, n]), (lambda j, n: ring_r.at[i, j, n])

    def columns(ref):
        return lambda t, r: ref.at[(*r, pl.ds(pl.multiple_of(t * 256, 256), 256))]

    def pieces(ref):
        return lambda t, r: ref.at[(t, *r)]

    kh = KC // 2
    g_ag = Gather("x", *ring_sems("g"), kh, lambda r: g_ref.at[r], columns(gx))
    t_rs = Scatter("z", *ring_sems("trs"), kh, pieces(tp), t_comb, t_fin, lambda r: tx.at[(x, *r)])
    t_ag = Gather("x", *ring_sems("tag"), kh, lambda r: tx.at[(x, *r)], pieces(tx))
    r_rs = Scatter("y", *ring_sems("rrs"), None, lambda t, r: pp.at[(c, t, *r)], r_comb, r_fin, lambda r: rot_own.at[r])
    d_ag = Gather("y", *ring_sems("dag"), None, lambda r: dall.at[(c, y, *r)], lambda t, r: dall.at[(c, t, *r)])
    b_rs = Scatter("x", *ring_sems("brs"), kh, pieces(blp), b_comb, b_fin, lambda r: columns(blz)(z, r))
    b_ag = Gather("z", *ring_sems("bag"), kh, lambda r: columns(blz)(z, r), columns(blz))
    u_rs = Scatter("x", *ring_sems("urs"), kh, pieces(up), u_comb, u_fin, lambda r: u_out.at[r])

    def l_unit(h, j):
        i = h * 2 + j

        def src(r):
            return l_ref.at[(*r, pl.ds(h * 256 + j * 128, 128))]

        def dst(t, r):
            return lh.at[(h, *r, pl.ds(pl.multiple_of(j * 512 + t * 128, 128), 128))]

        return Gather("z", lambda _, n: l_s.at[i, n], lambda _, n: l_r.at[i, n], 512, src, dst)

    l_units = [[l_unit(h, j) for h in range(2)] for j in range(2)]

    def rb_block(t, cc):
        return rb.at[pl.ds(pl.multiple_of(t * 256 + cc * 128, 128), 128)]

    def rb_rows(t, r):
        return rb.at[pl.ds(pl.multiple_of(t * 256 + c * 128 + r[0].start, 64), r[0].size)]

    r_ag = Gather("y", lambda _, n: ra_s.at[n], lambda _, n: ra_r.at[n], 64, lambda r: rb_rows(y, r), rb_rows)

    def rb_tile(cc, zz):
        return rb.at[
            pl.ds(pl.multiple_of(y * 256 + cc * 128, 128), 128), pl.ds(pl.multiple_of(zz * 256, 256), 256)
        ]

    for sl in range(2):
        for cc in range(2):
            mine = jnp.logical_and(2 * c + sl == z, c == cc)
            send_or_keep(
                mine, r_ref.at[pl.ds(sl * 256 + cc * 128, 128)], rb_tile(cc, z),
                r1_s.at[sl, cc], r1_r.at[z], dev(x, y, 2 * c + sl, cc), near.at[0],
            )
    g_ag.start(0)
    g_ag.start(1)
    for unit in l_units[0]:
        unit.start(0)
    own = [local(g_ref, gx.at[:, pl.ds(pl.multiple_of(x * 256, 256), 256)], 1)]
    for h in range(2):
        for j in range(2):
            own.append(local(
                l_ref.at[:, pl.ds(h * 256 + j * 128, 128)],
                lh.at[h, :, pl.ds(pl.multiple_of(j * 512 + z * 128, 128), 128)], 2 + h * 2 + j,
            ))
    moments = [local(fm_ref, fm, 6), local(sm_ref, sm, 7)]
    for zz in range(4):
        mine = jnp.logical_and(zz == z, z // 2 == c)
        arrived_or_kept(mine, rb_tile(c, zz), r1_s.at[0, 0], r1_r.at[zz])
    r_ag.start(0)

    def sib_block(t, n):
        send(rb_block(t, c), rb_block(t, c), rsib_s.at[n], rsib_r.at[n], sib)

    sib_block(y, 0)
    g_ag.mid(0)
    g_ag.start(2)
    g_ag.mid(1)
    g_ag.start(3)
    r_ag.mid(0)
    g_ag.mid(2)
    for unit in l_units[0]:
        unit.mid(0)
    g_ag.mid(3)
    r_ag.end(0)
    for n, t in enumerate((r_ag.left, r_ag.right, r_ag.opp)):
        sib_block(t, n + 1)
    for n, t in enumerate((y, r_ag.left, r_ag.right, r_ag.opp)):
        arrived(rb_block(t, other), rsib_s.at[n], rsib_r.at[n])

    def rotate_right(j):
        rows = pl.ds(j * KC, KC)

        def body(b, _):
            right = rb[:, pl.ds(pl.multiple_of(b * 256, 256), 256)]
            tp[b, rows] = jnp.dot(gx[rows], right, preferred_element_type=F32).astype(BF)
            return 0

        lax.fori_loop(0, 4, body, 0)

    for copy in own:
        copy.wait()

    def first(j):
        g_ag.end(j)
        rotate_right(j)
        t_rs.start(j)

    def second(j):
        t_rs.end(j)
        t_ag.start(j)

    first(0)
    first(1)
    t_rs.mid(0)
    first(2)
    t_rs.mid(1)
    first(3)
    t_rs.mid(2)
    second(0)
    t_rs.mid(3)
    for unit in l_units[1]:
        unit.start(0)
    second(1)
    t_ag.mid(0)
    second(2)
    t_ag.mid(1)
    second(3)
    t_ag.mid(2)
    t_ag.mid(3)
    for unit in l_units[1]:
        unit.mid(0)
    for j in range(NK):
        t_ag.end(j)

    def rotate_left(h, j):
        columns = pl.ds(j * 512, 512)

        def body(a, _):
            pp[h, a, j] = lax.dot_general(
                lh[h, :, columns], tx[a], (((0,), (0,)), ((), ())), preferred_element_type=F32
            ).astype(BF).reshape(4, 2, 64, 256)
            return 0

        lax.fori_loop(0, 4, body, 0)

    def rotate_left_both(j):
        for unit in l_units[j]:
            unit.end(0)
        rotate_left(other, j)
        for a in range(4):
            send(pp.at[other, a, j], qq.at[a, j], psib_s.at[j, a], psib_r.at[j, a], sib)
        rotate_left(c, j)

    def add_sibling(j):
        for a in range(4):
            arrived(qq.at[a, j], psib_s.at[j, a], psib_r.at[j, a])
            pp[c, a, j] = (pp[c, a, j].astype(F32) + qq[a, j].astype(F32)).astype(BF)
        r_rs.start(2 * j)
        r_rs.start(2 * j + 1)

    def home_rows(cc, q):
        return pl.ds(cc * 256 + q // 2 * 128 + q % 2 * 64, 64)

    def home_tile(ref, cc, s, q):
        return ref.at[
            pl.ds(pl.multiple_of(cc * 256 + q // 2 * 128 + q % 2 * 64, 64), 64),
            pl.ds(pl.multiple_of(s * 256, 256), 256),
        ]

    def to_home(q):
        r_rs.end(q)
        for d in range(4):
            zz = wrap(z + d)
            place = (rot_own.at[q // 2, zz, q % 2], home_tile(rot_home, c, lax.rem(z, 2), q),
                     fwd_s.at[q, d], fwd_r.at[q, lax.rem(z, 2) * 2 + c], dev(x, y, zz, z // 2))
            if d:
                send(*place)
            else:
                send_or_keep(z // 2 == c, *place)

    outs = []

    def moment_step(q):
        for s in range(2):
            for cc in range(2):
                mine = jnp.logical_and(2 * c + s == z, c == cc)
                arrived_or_kept(mine, home_tile(rot_home, cc, s, q), fwd_s.at[q, 0], fwd_r.at[q, s * 2 + cc])
        for h in range(2):
            rows = home_rows(h, q)
            rotated = rot_home[rows].astype(F32)
            first_new = 0.9 * fm[rows] + 0.1 * rotated
            second_new = 0.95 * sm[rows] + 0.05 * rotated * rotated
            fm[rows] = first_new
            sm[rows] = second_new
            d_home[rows] = (first_new / (jnp.sqrt(second_new) + 1e-08)).astype(BF)
        for h in range(2):
            for s in range(2):
                mine = jnp.logical_and(2 * c + s == z, c == h)
                send_or_keep(
                    mine, home_tile(d_home, h, s, q), dall.at[h, y, q // 2, z, q % 2],
                    back_s.at[q, h, s], back_r.at[q, z], dev(x, y, 2 * c + s, h),
                )

    def d_block(t, q, cc):
        return dall.at[cc, t, q // 2, :, q % 2]

    order = (y, d_ag.left, d_ag.right, d_ag.opp)

    def d_start(q):
        for zz in range(4):
            mine = jnp.logical_and(zz == z, z // 2 == c)
            arrived_or_kept(mine, dall.at[c, y, q // 2, zz, q % 2], back_s.at[q, 0, 0], back_r.at[q, zz])
        d_ag.start(q)
        send(d_block(y, q, c), d_block(y, q, c), dsib_s.at[q, 0], dsib_r.at[q, 0], sib)

    def d_end(q):
        d_ag.end(q)
        for n in (1, 2, 3):
            send(d_block(order[n], q, c), d_block(order[n], q, c), dsib_s.at[q, n], dsib_r.at[q, n], sib)

    def d_sibling(q):
        for n in range(4):
            arrived(d_block(order[n], q, other), dsib_s.at[q, n], dsib_r.at[q, n])

    rotate_left_both(0)
    add_sibling(0)
    r_rs.mid(0)
    rotate_left_both(1)
    r_rs.mid(1)
    for copy in moments:
        copy.wait()
    to_home(0)
    add_sibling(1)
    to_home(1)
    moment_step(0)
    r_rs.mid(2)
    moment_step(1)
    r_rs.mid(3)
    d_start(0)
    to_home(2)
    d_start(1)
    to_home(3)
    d_ag.mid(0)
    moment_step(2)
    d_ag.mid(1)
    moment_step(3)
    outs += [local(fm, fn_ref, 6), local(sm, sn_ref, 7)]
    d_start(2)
    d_end(0)
    d_start(3)
    d_end(1)
    d_ag.mid(2)
    d_ag.mid(3)
    d_end(2)
    d_end(3)
    for q in range(NQ):
        d_sibling(q)

    def rotate_back_left(j):
        rows = pl.ds(j * KC, KC)

        def body(a, _):
            total = jnp.dot(lh[0, rows], dall[0, a].reshape(1024, 256), preferred_element_type=F32)
            total = total + jnp.dot(lh[1, rows], dall[1, a].reshape(1024, 256), preferred_element_type=F32)
            blp[a, rows] = total.astype(BF)
            return 0

        lax.fori_loop(0, 4, body, 0)

    def rotate_back_right(j):
        rows = pl.ds(j * KC, KC)

        def body(t, _):
            right = rb[pl.ds(pl.multiple_of(t * 256, 256), 256)]
            up[t, rows] = lax.dot_general(
                blz[rows], right, (((1,), (1,)), ((), ())), preferred_element_type=F32
            ).astype(BF)
            return 0

        lax.fori_loop(0, 4, body, 0)

    def third(j):
        rotate_back_left(j)
        b_rs.start(j)

    def fourth(j):
        b_rs.end(j)
        b_ag.start(j)

    def fifth(j):
        b_ag.end(j)
        rotate_back_right(j)
        u_rs.start(j)

    def last(j):
        u_rs.end(j)
        rows = pl.ds(j * KC, KC)
        outs.append(local(u_out.at[rows], u_ref.at[rows], 8 + j))

    third(0)
    third(1)
    third(2)
    b_rs.mid(0)
    third(3)
    b_rs.mid(1)
    b_rs.mid(2)
    fourth(0)
    b_rs.mid(3)
    fourth(1)
    b_ag.mid(0)
    fourth(2)
    b_ag.mid(1)
    fourth(3)
    fifth(0)
    b_ag.mid(2)
    fifth(1)
    b_ag.mid(3)
    u_rs.mid(0)
    fifth(2)
    u_rs.mid(1)
    fifth(3)
    u_rs.mid(2)
    last(0)
    u_rs.mid(3)
    last(1)
    last(2)
    last(3)
    for copy in outs:
        copy.wait()
    for mine, copy in sent:
        if mine is None:
            copy.wait_send()
        else:
            @pl.when(jnp.logical_not(mine))
            def _(copy=copy):
                copy.wait_send()


def per_device(grad, basis_left, basis_right, first_moment, second_moment):
    dma = pltpu.SemaphoreType.DMA
    part = (2, 64, 256)
    m_rows = (2, 4, 2, 64, 256)

    def scatter_buffers(chunks, half):
        return [pltpu.VMEM((chunks, 2, *half), BF), pltpu.VMEM((chunks, 2, 2, *half), BF)]

    scratch = [
        pltpu.VMEM((1024, 1024), BF),
        pltpu.VMEM((1024, 1024), BF),
        pltpu.VMEM((4, 1024, 256), BF),
        pltpu.VMEM((4, 1024, 256), BF),
        pltpu.VMEM((2, 1024, 1024), BF),
        pltpu.VMEM((2, 4, *m_rows), BF),
        pltpu.VMEM((4, *m_rows), BF),
        pltpu.VMEM(m_rows, BF),
        pltpu.VMEM((512, 512), BF),
        pltpu.VMEM((512, 512), BF),
        pltpu.VMEM((2, 4, *m_rows), BF),
        pltpu.VMEM((4, 1024, 256), BF),
        pltpu.VMEM((1024, 1024), BF),
        pltpu.VMEM((4, 1024, 256), BF),
        pltpu.VMEM((1024, 256), BF),
        pltpu.VMEM((512, 512), F32),
        pltpu.VMEM((512, 512), F32),
    ]
    k_part = (KC // 2, 256)
    for chunks, half in ((NK, k_part), (NQ, part), (NK, k_part), (NK, k_part)):
        scratch += scatter_buffers(chunks, half)
    most = max(NK, NQ)
    for out, back in (
        ((len(OPS), most, 6), (len(OPS), most, 6)), ((4, 6), (4, 6)), ((6,), (6,)), ((2, 2), (4,)),
        ((4,), (4,)), ((2, 4), (2, 4)), ((NQ, 4), (NQ, 4)), ((NQ, 2, 2), (NQ, 4)), ((NQ, 4), (NQ, 4)),
    ):
        scratch += [dma(out), dma(back)]
    scratch.append(dma((8 + NK,)))
    anywhere = pl.BlockSpec(memory_space=pl.ANY)
    return pl.pallas_call(
        kernel,
        out_shape=(
            jax.ShapeDtypeStruct((1024, 256), BF),
            jax.ShapeDtypeStruct((512, 512), F32),
            jax.ShapeDtypeStruct((512, 512), F32),
        ),
        in_specs=[anywhere] * 5,
        out_specs=[anywhere] * 3,
        scratch_shapes=scratch,
        compiler_params=pltpu.CompilerParams(
            collective_id=0, has_side_effects=True, vmem_limit_bytes=60 * 1024 * 1024
        ),
        cost_estimate=pl.CostEstimate(flops=12884901888, bytes_accessed=6553600, transcendentals=262144),
    )(grad, basis_left, basis_right, first_moment, second_moment)


def solution(mesh):
    in_specs = (P("row", "col"), P("row", "col"), P("row", "col"), P("col", "row"), P("col", "row"))
    out_specs = (P("row", "col"), P("col", "row"), P("col", "row"))
    return jax.shard_map(
        per_device, mesh=mesh, in_specs=in_specs, out_specs=out_specs, check_vma=False
    )
```

```python
import functools

import jax
import jax.numpy as jnp
from jax import lax
from jax.experimental import pallas as pl
from jax.experimental.pallas import tpu as pltpu
from jax.sharding import PartitionSpec as P

MESH = pl.DeviceIdType.MESH
BF = jnp.bfloat16
F32 = jnp.float32
NJ = 4
NK = 4
KC = 1024 // NK
NG = 4


def wrap(v):
    return lax.rem(v + 8, 4)


def block(i, n):
    return pl.ds(pl.multiple_of(i * n, n), n)


def kernel(
    g_ref, l_ref, r_ref, fm_ref, sm_ref,
    u_ref, fn_ref, sn_ref,
    gz, lh, rr, lp, lq, lr, rp, rot, dx, ep, eq, ee, up, u_out, fm, sm,
    l_comb, l_fin, r_comb, r_fin, e_comb, e_fin, u_comb, u_fin,
    ring_s, ring_r, sib_r, turn_s, turn_r, cast_s, cast_r, near,
):
    row, col = lax.axis_index("row"), lax.axis_index("col")
    y, c, x, z = row // 2, lax.rem(row, 2), col // 4, lax.rem(col, 4)
    other = 1 - c

    def dev(x, y, z, c):
        return (y * 2 + c, x * 4 + z)

    sib = dev(x, y, z, other)
    ring = {
        "x": (x, dev(wrap(x + 1), y, z, c), dev(wrap(x - 1), y, z, c)),
        "y": (y, dev(x, wrap(y + 1), z, c), dev(x, wrap(y - 1), z, c)),
        "z": (z, dev(x, y, wrap(z + 1), c), dev(x, y, wrap(z - 1), c)),
    }

    barrier = pltpu.get_barrier_semaphore()
    partners = [*ring["x"][1:], *ring["y"][1:], *ring["z"][1:], dev(x, y, wrap(z + 2), c), sib]
    for partner in partners:
        pl.semaphore_signal(barrier, inc=1, device_id=partner, device_id_type=MESH)

    @pl.when(x != y)
    def _():
        for cc in range(2):
            pl.semaphore_signal(barrier, inc=1, device_id=dev(y, x, z, cc), device_id_type=MESH)

    pl.semaphore_wait(barrier, jnp.where(x != y, len(partners) + 2, len(partners)))

    def remote(src, dst, ssem, rsem, device):
        return pltpu.make_async_remote_copy(
            src_ref=src, dst_ref=dst, send_sem=ssem, recv_sem=rsem, device_id=device, device_id_type=MESH
        )

    def arrived(dst, rsem):
        remote(dst, dst, ring_s.at[0], rsem, sib).wait_recv()

    def local(src, dst, n):
        copy = pltpu.make_async_copy(src, dst, near.at[n])
        copy.start()
        return copy

    class Ring:
        count = 0
        sems = 0

        def __init__(self, axis, chunks, four):
            self.pos, self.right_dev, self.left_dev = ring[axis]
            self.right, self.left, self.opp = wrap(self.pos + 1), wrap(self.pos - 1), wrap(self.pos + 2)
            self.op, self.base, self.four = Ring.count, Ring.sems, four
            Ring.count += 1
            Ring.sems += 3 * chunks

        def rsem(self, j, n):
            return ring_r.at[self.base + 3 * j + {0: 0, 3: 1}.get(n, 2)]

        def go(self, j, n, src, dst):
            remote(src, dst, ring_s.at[self.op], self.rsem(j, n), self.right_dev if n < 3 else self.left_dev).start()

        def wait(self, j, n, dst):
            arrived(dst, self.rsem(j, n))

        def wait_four(self, j):
            arrived(self.four, self.rsem(j, 1))

    class Gather(Ring):
        def __init__(self, axis, chunks, four, src, dst):
            super().__init__(axis, chunks, four)
            self.src, self.dst = src, dst

        def start(self, j):
            self.go(j, 0, self.src(j, 0), self.dst(self.pos, j, 0))
            self.go(j, 3, self.src(j, 1), self.dst(self.pos, j, 1))
            self.go(j, 1, self.src(j, 1), self.dst(self.pos, j, 1))
            self.go(j, 4, self.src(j, 0), self.dst(self.pos, j, 0))

        def mid(self, j):
            self.wait(j, 0, self.dst(self.left, j, 0))
            self.go(j, 2, self.dst(self.left, j, 0), self.dst(self.left, j, 0))
            self.wait(j, 3, self.dst(self.right, j, 1))
            self.go(j, 5, self.dst(self.right, j, 1), self.dst(self.right, j, 1))

        def end(self, j):
            self.wait_four(j)

    class Scatter(Ring):
        def __init__(self, axis, chunks, four, piece, comb, fin, out):
            super().__init__(axis, chunks, four)
            self.piece, self.comb, self.fin, self.out = piece, comb, fin, out

        def start(self, j):
            self.go(j, 0, self.piece(self.opp, j, 0), self.comb.at[j, 0])
            self.go(j, 3, self.piece(self.opp, j, 1), self.comb.at[j, 1])
            self.go(j, 1, self.piece(self.right, j, 1), self.fin.at[j, 0, 1])
            self.go(j, 4, self.piece(self.left, j, 0), self.fin.at[j, 1, 0])

        def mid(self, j):
            for n, side, h in ((0, self.right, 0), (3, self.left, 1)):
                self.wait(j, n, self.comb.at[j, h])
                ref = self.piece(side, j, h)
                ref[...] = (ref[...].astype(F32) + self.comb[j, h].astype(F32)).astype(BF)
                self.go(j, n + 2, ref, self.fin.at[j, h, h])

        def end(self, j):
            self.wait_four(j)
            for h in range(2):
                total = self.piece(self.pos, j, h)[...].astype(F32)
                total = total + self.fin[j, 0, h].astype(F32) + self.fin[j, 1, h].astype(F32)
                self.out(j, h)[...] = total.astype(BF)

    def half_columns(ref):
        return lambda t, j, h: ref.at[j, pl.ds(2 * h, 2), c, :, block(t, 256)]

    def half_pieces(ref):
        return lambda t, j, h: ref.at[j, t, pl.ds(2 * h, 2), c]

    gh, kh = 1024 // NG // 2, KC // 2
    g_ag = Gather(
        "z", NG, lp.at[0, 0],
        lambda j, h: g_ref.at[pl.ds((2 * j + h) * gh, gh)],
        lambda t, j, h: gz.at[pl.ds((2 * j + h) * gh, gh), block(t, 256)],
    )
    l_ag = Gather(
        "x", NJ, lp.at[0, pl.ds(0, 2)],
        lambda j, h: l_ref.at[pl.ds(h * 512, 512), pl.ds(j * 128, 128)],
        lambda t, j, h: lh.at[j, pl.ds(h * 512, 512), block(t, 128)],
    )
    quarter = lp.at[0, 0]
    lr_rs = Scatter("y", NJ, quarter, half_pieces(lp), l_comb, l_fin, lambda j, h: half_columns(lr)(y, j, h))
    lr_ag = Gather("y", NJ, quarter, lambda j, h: half_columns(lr)(y, j, h), half_columns(lr))
    rot_rs = Scatter(
        "x", NJ, quarter, lambda t, j, h: rp.at[j, t, h], r_comb, r_fin,
        lambda j, h: rot.at[pl.ds(j * 128 + h * 64, 64)],
    )
    d_ag = Gather("x", NJ, quarter, lambda j, h: dx.at[j, x, h], lambda t, j, h: dx.at[j, t, h])
    e_rs = Scatter("y", NJ, quarter, half_pieces(ep), e_comb, e_fin, lambda j, h: half_columns(ee)(y, j, h))
    e_ag = Gather("y", NJ, quarter, lambda j, h: half_columns(ee)(y, j, h), half_columns(ee))
    u_rs = Scatter(
        "z", NK, quarter, lambda t, j, h: up.at[t, pl.ds(j * KC + h * kh, kh)], u_comb, u_fin,
        lambda j, h: u_out.at[pl.ds(j * KC + h * kh, kh)],
    )
    class Total:
        def __init__(self, rs, ag, parts, theirs, full, first):
            self.rs, self.ag, self.parts, self.theirs, self.full, self.first = rs, ag, parts, theirs, full, first
            self.ssem = ring_s.at[Ring.count + first // (2 * NJ)]

        def swap(self, j):
            remote(
                self.parts.at[j, :, :, other], self.theirs.at[j], self.ssem, sib_r.at[self.first + j], sib
            ).start()

        def add(self, j):
            arrived(self.theirs.at[j], sib_r.at[self.first + j])
            for t in range(4):
                mine = self.parts[j, t, :, c].astype(F32)
                self.parts[j, t, :, c] = (mine + self.theirs[j, t].astype(F32)).astype(BF)
            self.rs.start(j)

        def share(self, j, t):
            ref = self.full.at[j, :, c, :, block(t, 256)]
            remote(ref, ref, self.ssem, sib_r.at[self.first + NJ + j], sib).start()

        def turn(self, j):
            self.rs.end(j)
            self.ag.start(j)
            self.share(j, y)

        def end(self, j):
            self.ag.end(j)
            for t in (self.ag.left, self.ag.right, self.ag.opp):
                self.share(j, t)

        def ready(self, j):
            arrived(self.full.at[j, :, other], sib_r.at[self.first + NJ + j])

    lr_sum = Total(lr_rs, lr_ag, lp, lq, lr, 0)
    e_sum = Total(e_rs, e_ag, ep, eq, ee, 2 * NJ)

    root = z // 2 == c
    keep = jnp.logical_and(x == y, root)
    cols_here = block(lax.rem(z, 2), 256)
    turned = remote(r_ref, rr.at[block(c, 512), cols_here], turn_s.at[0], turn_r.at[c], dev(y, x, z, z // 2))
    casts = [
        remote(rr.at[:, cols_here], rr.at[:, cols_here], cast_s.at[d - 1], cast_r.at[lax.rem(z, 2)], dev(x, y, wrap(z + d), c))
        for d in (1, 2, 3)
    ]

    def right_send():
        @pl.when(jnp.logical_not(keep))
        def _():
            turned.start()

        @pl.when(keep)
        def _():
            pltpu.make_async_copy(r_ref, rr.at[block(c, 512), cols_here], near.at[0]).start()

    def right_cast():
        @pl.when(root)
        def _():
            for cc in range(2):
                here = jnp.logical_and(x == y, c == cc)

                @pl.when(here)
                def _():
                    pltpu.make_async_copy(r_ref, rr.at[pl.ds(cc * 512, 512), cols_here], near.at[0]).wait()

                @pl.when(jnp.logical_not(here))
                def _():
                    arrived(rr.at[pl.ds(cc * 512, 512), cols_here], turn_r.at[cc])

            for cast in casts:
                cast.start()

    def right_ready():
        for s in range(2):
            @pl.when(2 * c + s != z)
            def _():
                arrived(rr.at[:, pl.ds(s * 256, 256)], cast_r.at[s])

    def left_product(j):
        def body(t, _):
            lp[j, t] = lax.dot_general(
                lh[j], gz[:, block(t, 256)], (((0,), (0,)), ((), ())), preferred_element_type=F32
            ).astype(BF).reshape(4, 2, 64, 256)
            return 0

        lax.fori_loop(0, 4, body, 0)
        lr_sum.swap(j)

    def right_product(j):
        lr_sum.ready(j)
        rp[j] = jnp.dot(
            lr[j].reshape(512, 1024), rr[...], preferred_element_type=F32
        ).astype(BF).reshape(4, 2, 64, 512)
        rot_rs.start(j)

    outs = []

    def moment_step(j):
        rot_rs.end(j)
        for h in range(2):
            rows = pl.ds(j * 128 + h * 64, 64)
            rotated = rot[rows].astype(F32)
            first_new = 0.9 * fm[rows] + 0.1 * rotated
            second_new = 0.95 * sm[rows] + 0.05 * rotated * rotated
            fm[rows] = first_new
            sm[rows] = second_new
            dx[j, x, h] = (first_new / (jnp.sqrt(second_new) + 1e-08)).astype(BF)
        d_ag.start(j)

    def right_back(j):
        d_ag.end(j)

        def body(t, _):
            ep[j, t] = lax.dot_general(
                dx[j].reshape(512, 512), rr[block(t, 256)], (((1,), (1,)), ((), ())), preferred_element_type=F32
            ).astype(BF).reshape(4, 2, 64, 256)
            return 0

        lax.fori_loop(0, 4, body, 0)
        e_sum.swap(j)

    def left_back(k):
        rows = pl.ds(k * KC, KC)

        def body(t, _):
            total = jnp.zeros((KC, 256), F32)
            for j in range(NJ):
                right = ee[j, :, :, :, block(t, 256)].reshape(512, 256)
                total = total + jnp.dot(lh[j, rows], right, preferred_element_type=F32)
            up[t, rows] = total.astype(BF)
            return 0

        lax.fori_loop(0, 4, body, 0)
        u_rs.start(k)

    def last(k):
        u_rs.end(k)
        rows = pl.ds(k * KC, KC)
        outs.append(local(u_out.at[rows], u_ref.at[rows], 4 + k))

    l_ag.start(0)
    l_ag.start(1)
    g_ag.start(0)
    own = [local(g_ref, gz.at[:, block(z, 256)], 1)]
    for j in range(4):
        own.append(local(l_ref.at[:, pl.ds(j * 128, 128)], lh.at[j, :, block(x, 128)], 4 + j))
    moments = [local(fm_ref, fm, 2), local(sm_ref, sm, 3)]
    g_ag.mid(0)
    g_ag.start(1)
    g_ag.start(2)
    g_ag.start(3)
    l_ag.mid(0)
    g_ag.mid(1)
    l_ag.mid(1)
    g_ag.mid(2)
    right_send()
    l_ag.start(2)
    l_ag.start(3)
    g_ag.mid(3)
    for copy in own:
        copy.wait()
    l_ag.end(1)
    g_ag.end(0)
    g_ag.end(1)
    g_ag.end(2)
    g_ag.end(3)
    left_product(1)
    lr_sum.add(1)
    l_ag.end(0)
    left_product(0)
    right_cast()
    lr_rs.mid(1)
    lr_sum.add(0)
    lr_sum.turn(1)
    lr_rs.mid(0)
    l_ag.mid(3)
    l_ag.mid(2)
    lr_ag.mid(1)
    lr_sum.turn(0)
    lr_sum.end(1)
    l_ag.end(3)
    left_product(3)
    right_ready()
    right_product(1)
    lr_ag.mid(0)
    l_ag.end(2)
    left_product(2)
    lr_sum.add(3)
    rot_rs.mid(1)
    lr_sum.end(0)
    right_product(0)
    lr_rs.mid(3)
    lr_sum.add(2)
    for copy in moments:
        copy.wait()
    moment_step(1)
    rot_rs.mid(0)
    lr_sum.turn(3)
    lr_rs.mid(2)
    d_ag.mid(1)
    lr_ag.mid(3)
    moment_step(0)
    lr_sum.turn(2)
    right_back(1)
    lr_sum.end(3)
    d_ag.mid(0)
    lr_ag.mid(2)
    e_sum.add(1)
    right_product(3)
    lr_sum.end(2)
    right_back(0)
    rot_rs.mid(3)
    right_product(2)
    e_sum.add(0)
    moment_step(3)
    rot_rs.mid(2)
    e_rs.mid(1)
    e_rs.mid(0)
    d_ag.mid(3)
    e_sum.turn(1)
    moment_step(2)
    outs += [local(fm, fn_ref, 2), local(sm, sn_ref, 3)]
    e_sum.turn(0)
    right_back(3)
    e_ag.mid(1)
    d_ag.mid(2)
    e_sum.add(3)
    e_ag.mid(0)
    right_back(2)
    e_rs.mid(3)
    e_sum.add(2)
    e_sum.end(0)
    e_rs.mid(2)
    e_sum.turn(3)
    e_sum.end(1)
    e_sum.turn(2)
    e_ag.mid(3)
    e_ag.mid(2)
    e_sum.end(3)
    e_sum.end(2)
    for j in range(NJ):
        e_sum.ready(j)
    left_back(1)
    left_back(3)
    left_back(0)
    u_rs.mid(1)
    left_back(2)
    u_rs.mid(3)
    u_rs.mid(0)
    last(1)
    u_rs.mid(2)
    last(3)
    last(0)
    last(2)
    for copy in outs:
        copy.wait()

    for op in range(Ring.count):
        whole = lp.at[pl.ds(0, 3)] if op == l_ag.op else lp.at[pl.ds(0, 3), pl.ds(0, 2)]
        remote(whole, whole, ring_s.at[op], ring_r.at[0], sib).wait_send()
    for total in (lr_sum, e_sum):
        remote(lh, lh, total.ssem, ring_r.at[0], sib).wait_send()

    @pl.when(jnp.logical_not(keep))
    def _():
        turned.wait_send()

    @pl.when(root)
    def _():
        for cast in casts:
            cast.wait_send()


def per_device(grad, basis_left, basis_right, first_moment, second_moment):
    dma = pltpu.SemaphoreType.DMA

    def scatter_buffers(chunks, half):
        return [pltpu.VMEM((chunks, 2, *half), BF), pltpu.VMEM((chunks, 2, 2, *half), BF)]

    scratch = [
        pltpu.VMEM((1024, 1024), BF),
        pltpu.VMEM((NJ, 1024, 512), BF),
        pltpu.VMEM((1024, 512), BF),
        pltpu.VMEM((NJ, 4, 4, 2, 64, 256), BF),
        pltpu.VMEM((NJ, 4, 4, 64, 256), BF),
        pltpu.VMEM((NJ, 4, 2, 64, 1024), BF),
        pltpu.VMEM((NJ, 4, 2, 64, 512), BF),
        pltpu.VMEM((512, 512), BF),
        pltpu.VMEM((NJ, 4, 2, 64, 512), BF),
        pltpu.VMEM((NJ, 4, 4, 2, 64, 256), BF),
        pltpu.VMEM((NJ, 4, 4, 64, 256), BF),
        pltpu.VMEM((NJ, 4, 2, 64, 1024), BF),
        pltpu.VMEM((4, 1024, 256), BF),
        pltpu.VMEM((1024, 256), BF),
        pltpu.VMEM((512, 512), F32),
        pltpu.VMEM((512, 512), F32),
    ]
    for chunks, half in ((NJ, (2, 64, 256)), (NJ, (64, 512)), (NJ, (2, 64, 256)), (NK, (KC // 2, 256))):
        scratch += scatter_buffers(chunks, half)
    scratch += [dma((n,)) for n in (11, 3 * (NG + 7 * NJ + NK), 4 * NJ, 1, 2, 3, 2, 8)]
    anywhere = pl.BlockSpec(memory_space=pl.ANY)
    return pl.pallas_call(
        kernel,
        out_shape=(
            jax.ShapeDtypeStruct((1024, 256), BF),
            jax.ShapeDtypeStruct((512, 512), F32),
            jax.ShapeDtypeStruct((512, 512), F32),
        ),
        in_specs=[anywhere] * 5,
        out_specs=[anywhere] * 3,
        scratch_shapes=scratch,
        compiler_params=pltpu.CompilerParams(
            collective_id=0, has_side_effects=True, vmem_limit_bytes=60 * 1024 * 1024
        ),
        cost_estimate=pl.CostEstimate(flops=12884901888, bytes_accessed=6553600, transcendentals=262144),
    )(grad, basis_left, basis_right, first_moment, second_moment)


def solution(mesh):
    in_specs = (P("row", "col"), P("row", "col"), P("row", "col"), P("col", "row"), P("col", "row"))
    out_specs = (P("row", "col"), P("col", "row"), P("col", "row"))
    return jax.shard_map(
        per_device, mesh=mesh, in_specs=in_specs, out_specs=out_specs, check_vma=False
    )
```

```python
import functools

import jax
import jax.numpy as jnp
from jax import lax
from jax.experimental import pallas as pl
from jax.experimental.pallas import tpu as pltpu
from jax.sharding import PartitionSpec as P

MESH = pl.DeviceIdType.MESH
BF = jnp.bfloat16
F32 = jnp.float32
NJ = 4
NK = 4
KC = 1024 // NK
NG = 4


def wrap(v):
    return lax.rem(v + 8, 4)


def block(i, n):
    return pl.ds(pl.multiple_of(i * n, n), n)


def kernel(
    g_ref, l_ref, r_ref, fm_ref, sm_ref,
    u_ref, fn_ref, sn_ref,
    gz, lh, rr, lp, lq, lr, rp, rot, dx, ep, eq, ee, up, u_out, fm, sm,
    l_comb, l_fin, r_comb, r_fin, e_comb, e_fin, u_comb, u_fin,
    ring_s, ring_r, sib_r, turn_s, turn_r, cast_s, cast_r, near,
):
    row, col = lax.axis_index("row"), lax.axis_index("col")
    y, c, x, z = row // 2, lax.rem(row, 2), col // 4, lax.rem(col, 4)
    other = 1 - c

    def dev(x, y, z, c):
        return (y * 2 + c, x * 4 + z)

    sib = dev(x, y, z, other)
    ring = {
        "x": (x, dev(wrap(x + 1), y, z, c), dev(wrap(x - 1), y, z, c)),
        "y": (y, dev(x, wrap(y + 1), z, c), dev(x, wrap(y - 1), z, c)),
        "z": (z, dev(x, y, wrap(z + 1), c), dev(x, y, wrap(z - 1), c)),
    }

    barrier = pltpu.get_barrier_semaphore()
    partners = [*ring["x"][1:], *ring["y"][1:], *ring["z"][1:], dev(x, y, wrap(z + 2), c), sib]
    for partner in partners:
        pl.semaphore_signal(barrier, inc=1, device_id=partner, device_id_type=MESH)

    @pl.when(x != y)
    def _():
        for cc in range(2):
            pl.semaphore_signal(barrier, inc=1, device_id=dev(y, x, z, cc), device_id_type=MESH)

    pl.semaphore_wait(barrier, jnp.where(x != y, len(partners) + 2, len(partners)))

    def remote(src, dst, ssem, rsem, device):
        return pltpu.make_async_remote_copy(
            src_ref=src, dst_ref=dst, send_sem=ssem, recv_sem=rsem, device_id=device, device_id_type=MESH
        )

    def arrived(dst, rsem):
        remote(dst, dst, ring_s.at[0], rsem, sib).wait_recv()

    def local(src, dst, n):
        copy = pltpu.make_async_copy(src, dst, near.at[n])
        copy.start()
        return copy

    class Ring:
        count = 0
        sems = 0

        def __init__(self, axis, chunks, four):
            self.pos, self.right_dev, self.left_dev = ring[axis]
            self.right, self.left, self.opp = wrap(self.pos + 1), wrap(self.pos - 1), wrap(self.pos + 2)
            self.op, self.base, self.four = Ring.count, Ring.sems, four
            Ring.count += 1
            Ring.sems += 3 * chunks

        def rsem(self, j, n):
            return ring_r.at[self.base + 3 * j + {0: 0, 3: 1}.get(n, 2)]

        def go(self, j, n, src, dst):
            remote(src, dst, ring_s.at[self.op], self.rsem(j, n), self.right_dev if n < 3 else self.left_dev).start()

        def wait(self, j, n, dst):
            arrived(dst, self.rsem(j, n))

        def wait_four(self, j):
            arrived(self.four, self.rsem(j, 1))

    class Gather(Ring):
        def __init__(self, axis, chunks, four, src, dst):
            super().__init__(axis, chunks, four)
            self.src, self.dst = src, dst

        def start(self, j):
            self.go(j, 0, self.src(j, 0), self.dst(self.pos, j, 0))
            self.go(j, 3, self.src(j, 1), self.dst(self.pos, j, 1))
            self.go(j, 1, self.src(j, 1), self.dst(self.pos, j, 1))
            self.go(j, 4, self.src(j, 0), self.dst(self.pos, j, 0))

        def mid(self, j):
            self.wait(j, 0, self.dst(self.left, j, 0))
            self.go(j, 2, self.dst(self.left, j, 0), self.dst(self.left, j, 0))
            self.wait(j, 3, self.dst(self.right, j, 1))
            self.go(j, 5, self.dst(self.right, j, 1), self.dst(self.right, j, 1))

        def end(self, j):
            self.wait_four(j)

    class Scatter(Ring):
        def __init__(self, axis, chunks, four, piece, comb, fin, out):
            super().__init__(axis, chunks, four)
            self.piece, self.comb, self.fin, self.out = piece, comb, fin, out

        def start(self, j):
            self.go(j, 0, self.piece(self.opp, j, 0), self.comb.at[j, 0])
            self.go(j, 3, self.piece(self.opp, j, 1), self.comb.at[j, 1])
            self.go(j, 1, self.piece(self.right, j, 1), self.fin.at[j, 0, 1])
            self.go(j, 4, self.piece(self.left, j, 0), self.fin.at[j, 1, 0])

        def mid(self, j):
            for n, side, h in ((0, self.right, 0), (3, self.left, 1)):
                self.wait(j, n, self.comb.at[j, h])
                ref = self.piece(side, j, h)
                ref[...] = (ref[...].astype(F32) + self.comb[j, h].astype(F32)).astype(BF)
                self.go(j, n + 2, ref, self.fin.at[j, h, h])

        def end(self, j):
            self.wait_four(j)
            for h in range(2):
                total = self.piece(self.pos, j, h)[...].astype(F32)
                total = total + self.fin[j, 0, h].astype(F32) + self.fin[j, 1, h].astype(F32)
                self.out(j, h)[...] = total.astype(BF)

    def half_columns(ref):
        return lambda t, j, h: ref.at[j, pl.ds(2 * h, 2), c, :, block(t, 256)]

    def half_pieces(ref):
        return lambda t, j, h: ref.at[j, t, pl.ds(2 * h, 2), c]

    gh, kh = 1024 // NG // 2, KC // 2
    g_ag = Gather(
        "z", NG, lp.at[0, 0],
        lambda j, h: g_ref.at[pl.ds((2 * j + h) * gh, gh)],
        lambda t, j, h: gz.at[pl.ds((2 * j + h) * gh, gh), block(t, 256)],
    )
    l_ag = Gather(
        "x", NJ, lp.at[0, pl.ds(0, 2)],
        lambda j, h: l_ref.at[pl.ds(h * 512, 512), pl.ds(j * 128, 128)],
        lambda t, j, h: lh.at[j, pl.ds(h * 512, 512), block(t, 128)],
    )
    quarter = lp.at[0, 0]
    lr_rs = Scatter("y", NJ, quarter, half_pieces(lp), l_comb, l_fin, lambda j, h: half_columns(lr)(y, j, h))
    lr_ag = Gather("y", NJ, quarter, lambda j, h: half_columns(lr)(y, j, h), half_columns(lr))
    rot_rs = Scatter(
        "x", NJ, quarter, lambda t, j, h: rp.at[j, t, h], r_comb, r_fin,
        lambda j, h: rot.at[pl.ds(j * 128 + h * 64, 64)],
    )
    d_ag = Gather("x", NJ, quarter, lambda j, h: dx.at[j, x, h], lambda t, j, h: dx.at[j, t, h])
    e_rs = Scatter("y", NJ, quarter, half_pieces(ep), e_comb, e_fin, lambda j, h: half_columns(ee)(y, j, h))
    e_ag = Gather("y", NJ, quarter, lambda j, h: half_columns(ee)(y, j, h), half_columns(ee))
    u_rs = Scatter(
        "z", NK, quarter, lambda t, j, h: up.at[t, pl.ds(j * KC + h * kh, kh)], u_comb, u_fin,
        lambda j, h: u_out.at[pl.ds(j * KC + h * kh, kh)],
    )
    class Total:
        def __init__(self, rs, ag, parts, theirs, full, first):
            self.rs, self.ag, self.parts, self.theirs, self.full, self.first = rs, ag, parts, theirs, full, first
            self.ssem = ring_s.at[Ring.count + first // (2 * NJ)]

        def swap(self, j):
            remote(
                self.parts.at[j, :, :, other], self.theirs.at[j], self.ssem, sib_r.at[self.first + j], sib
            ).start()

        def add(self, j):
            arrived(self.theirs.at[j], sib_r.at[self.first + j])
            for t in range(4):
                mine = self.parts[j, t, :, c].astype(F32)
                self.parts[j, t, :, c] = (mine + self.theirs[j, t].astype(F32)).astype(BF)
            self.rs.start(j)

        def share(self, j, t):
            ref = self.full.at[j, :, c, :, block(t, 256)]
            remote(ref, ref, self.ssem, sib_r.at[self.first + NJ + j], sib).start()

        def turn(self, j):
            self.rs.end(j)
            self.ag.start(j)
            self.share(j, y)

        def end(self, j):
            self.ag.end(j)
            for t in (self.ag.left, self.ag.right, self.ag.opp):
                self.share(j, t)

        def ready(self, j):
            arrived(self.full.at[j, :, other], sib_r.at[self.first + NJ + j])

    lr_sum = Total(lr_rs, lr_ag, lp, lq, lr, 0)
    e_sum = Total(e_rs, e_ag, ep, eq, ee, 2 * NJ)

    root = z // 2 == c
    keep = jnp.logical_and(x == y, root)
    cols_here = block(lax.rem(z, 2), 256)
    turned = remote(r_ref, rr.at[block(c, 512), cols_here], turn_s.at[0], turn_r.at[c], dev(y, x, z, z // 2))
    casts = [
        remote(rr.at[:, cols_here], rr.at[:, cols_here], cast_s.at[d - 1], cast_r.at[lax.rem(z, 2)], dev(x, y, wrap(z + d), c))
        for d in (1, 2, 3)
    ]

    def right_send():
        @pl.when(jnp.logical_not(keep))
        def _():
            turned.start()

        @pl.when(keep)
        def _():
            pltpu.make_async_copy(r_ref, rr.at[block(c, 512), cols_here], near.at[0]).start()

    def right_cast():
        @pl.when(root)
        def _():
            for cc in range(2):
                here = jnp.logical_and(x == y, c == cc)

                @pl.when(here)
                def _():
                    pltpu.make_async_copy(r_ref, rr.at[pl.ds(cc * 512, 512), cols_here], near.at[0]).wait()

                @pl.when(jnp.logical_not(here))
                def _():
                    arrived(rr.at[pl.ds(cc * 512, 512), cols_here], turn_r.at[cc])

            for cast in casts:
                cast.start()

    def right_ready():
        for s in range(2):
            @pl.when(2 * c + s != z)
            def _():
                arrived(rr.at[:, pl.ds(s * 256, 256)], cast_r.at[s])

    def left_product(j):
        part = lax.dot_general(lh[j], gz[...], (((0,), (0,)), ((), ())), preferred_element_type=F32).astype(BF)
        for t in range(4):
            lp[j, t] = part[:, t * 256 : t * 256 + 256].reshape(4, 2, 64, 256)
        lr_sum.swap(j)

    def right_product(j):
        lr_sum.ready(j)
        rp[j] = jnp.dot(
            lr[j].reshape(512, 1024), rr[...], preferred_element_type=F32
        ).astype(BF).reshape(4, 2, 64, 512)
        rot_rs.start(j)

    outs = []

    def moment_step(j):
        rot_rs.end(j)
        for h in range(2):
            rows = pl.ds(j * 128 + h * 64, 64)
            rotated = rot[rows].astype(F32)
            first_new = 0.9 * fm[rows] + 0.1 * rotated
            second_new = 0.95 * sm[rows] + 0.05 * rotated * rotated
            fm[rows] = first_new
            sm[rows] = second_new
            dx[j, x, h] = (first_new / (jnp.sqrt(second_new) + 1e-08)).astype(BF)
        d_ag.start(j)

    def right_back(j):
        d_ag.end(j)

        part = lax.dot_general(
            dx[j].reshape(512, 512), rr[...], (((1,), (1,)), ((), ())), preferred_element_type=F32
        ).astype(BF)
        for t in range(4):
            ep[j, t] = part[:, t * 256 : t * 256 + 256].reshape(4, 2, 64, 256)
        e_sum.swap(j)

    def left_back(k):
        rows = pl.ds(k * KC, KC)

        total = jnp.dot(lh[0, rows], ee[0].reshape(512, 1024), preferred_element_type=F32)
        for j in range(1, NJ):
            total = total + jnp.dot(lh[j, rows], ee[j].reshape(512, 1024), preferred_element_type=F32)
        for t in range(4):
            up[t, rows] = total[:, t * 256 : t * 256 + 256].astype(BF)
        u_rs.start(k)

    def last(k):
        u_rs.end(k)
        rows = pl.ds(k * KC, KC)
        outs.append(local(u_out.at[rows], u_ref.at[rows], 4 + k))

    l_ag.start(0)
    l_ag.start(1)
    g_ag.start(0)
    own = [local(g_ref, gz.at[:, block(z, 256)], 1)]
    for j in range(4):
        own.append(local(l_ref.at[:, pl.ds(j * 128, 128)], lh.at[j, :, block(x, 128)], 4 + j))
    moments = [local(fm_ref, fm, 2), local(sm_ref, sm, 3)]
    g_ag.mid(0)
    g_ag.start(1)
    g_ag.start(2)
    g_ag.start(3)
    l_ag.mid(0)
    g_ag.mid(1)
    l_ag.mid(1)
    g_ag.mid(2)
    right_send()
    l_ag.start(2)
    l_ag.start(3)
    g_ag.mid(3)
    for copy in own:
        copy.wait()
    l_ag.end(1)
    g_ag.end(0)
    g_ag.end(1)
    g_ag.end(2)
    g_ag.end(3)
    left_product(1)
    lr_sum.add(1)
    l_ag.end(0)
    left_product(0)
    right_cast()
    lr_rs.mid(1)
    lr_sum.add(0)
    lr_sum.turn(1)
    lr_rs.mid(0)
    l_ag.mid(3)
    l_ag.mid(2)
    lr_ag.mid(1)
    lr_sum.turn(0)
    lr_sum.end(1)
    l_ag.end(3)
    left_product(3)
    right_ready()
    right_product(1)
    lr_ag.mid(0)
    l_ag.end(2)
    left_product(2)
    lr_sum.add(3)
    rot_rs.mid(1)
    lr_sum.end(0)
    right_product(0)
    lr_rs.mid(3)
    lr_sum.add(2)
    for copy in moments:
        copy.wait()
    moment_step(1)
    rot_rs.mid(0)
    lr_sum.turn(3)
    lr_rs.mid(2)
    d_ag.mid(1)
    lr_ag.mid(3)
    moment_step(0)
    lr_sum.turn(2)
    right_back(1)
    lr_sum.end(3)
    d_ag.mid(0)
    lr_ag.mid(2)
    e_sum.add(1)
    right_product(3)
    lr_sum.end(2)
    right_back(0)
    rot_rs.mid(3)
    right_product(2)
    e_sum.add(0)
    moment_step(3)
    rot_rs.mid(2)
    e_rs.mid(1)
    e_rs.mid(0)
    d_ag.mid(3)
    e_sum.turn(1)
    moment_step(2)
    outs += [local(fm, fn_ref, 2), local(sm, sn_ref, 3)]
    e_sum.turn(0)
    right_back(3)
    e_ag.mid(1)
    d_ag.mid(2)
    e_sum.add(3)
    e_ag.mid(0)
    right_back(2)
    e_rs.mid(3)
    e_sum.add(2)
    e_sum.end(0)
    e_rs.mid(2)
    e_sum.turn(3)
    e_sum.end(1)
    e_sum.turn(2)
    e_ag.mid(3)
    e_ag.mid(2)
    e_sum.end(3)
    e_sum.end(2)
    for j in range(NJ):
        e_sum.ready(j)
    left_back(1)
    left_back(3)
    left_back(0)
    u_rs.mid(1)
    left_back(2)
    u_rs.mid(3)
    u_rs.mid(0)
    last(1)
    u_rs.mid(2)
    last(3)
    last(0)
    last(2)
    for copy in outs:
        copy.wait()

    for op in range(Ring.count):
        whole = lp.at[pl.ds(0, 3)] if op == l_ag.op else lp.at[pl.ds(0, 3), pl.ds(0, 2)]
        remote(whole, whole, ring_s.at[op], ring_r.at[0], sib).wait_send()
    for total in (lr_sum, e_sum):
        remote(lh, lh, total.ssem, ring_r.at[0], sib).wait_send()

    @pl.when(jnp.logical_not(keep))
    def _():
        turned.wait_send()

    @pl.when(root)
    def _():
        for cast in casts:
            cast.wait_send()


def per_device(grad, basis_left, basis_right, first_moment, second_moment):
    dma = pltpu.SemaphoreType.DMA

    def scatter_buffers(chunks, half):
        return [pltpu.VMEM((chunks, 2, *half), BF), pltpu.VMEM((chunks, 2, 2, *half), BF)]

    scratch = [
        pltpu.VMEM((1024, 1024), BF),
        pltpu.VMEM((NJ, 1024, 512), BF),
        pltpu.VMEM((1024, 512), BF),
        pltpu.VMEM((NJ, 4, 4, 2, 64, 256), BF),
        pltpu.VMEM((NJ, 4, 4, 64, 256), BF),
        pltpu.VMEM((NJ, 4, 2, 64, 1024), BF),
        pltpu.VMEM((NJ, 4, 2, 64, 512), BF),
        pltpu.VMEM((512, 512), BF),
        pltpu.VMEM((NJ, 4, 2, 64, 512), BF),
        pltpu.VMEM((NJ, 4, 4, 2, 64, 256), BF),
        pltpu.VMEM((NJ, 4, 4, 64, 256), BF),
        pltpu.VMEM((NJ, 4, 2, 64, 1024), BF),
        pltpu.VMEM((4, 1024, 256), BF),
        pltpu.VMEM((1024, 256), BF),
        pltpu.VMEM((512, 512), F32),
        pltpu.VMEM((512, 512), F32),
    ]
    for chunks, half in ((NJ, (2, 64, 256)), (NJ, (64, 512)), (NJ, (2, 64, 256)), (NK, (KC // 2, 256))):
        scratch += scatter_buffers(chunks, half)
    scratch += [dma((n,)) for n in (11, 3 * (NG + 7 * NJ + NK), 4 * NJ, 1, 2, 3, 2, 8)]
    anywhere = pl.BlockSpec(memory_space=pl.ANY)
    results = pl.pallas_call(
        kernel,
        out_shape=(
            jax.ShapeDtypeStruct((1024, 256), BF),
            jax.ShapeDtypeStruct((512, 512), F32),
            jax.ShapeDtypeStruct((512, 512), F32),
        ),
        in_specs=[anywhere] * 5,
        out_specs=[anywhere] * 3,
        scratch_shapes=scratch,
        compiler_params=pltpu.CompilerParams(
            collective_id=0, has_side_effects=True, vmem_limit_bytes=60 * 1024 * 1024
        ),
        cost_estimate=pl.CostEstimate(flops=12884901888, bytes_accessed=6553600, transcendentals=262144),
    )(grad, basis_left, basis_right, first_moment, second_moment)

    def hand_over(u, fn, sn, u_out, fn_out, sn_out, u_held, fn_held, sn_held, sems):
        steps = []
        for i, (src, held, dst) in enumerate(((u, u_held, u_out), (fn, fn_held, fn_out), (sn, sn_held, sn_out))):
            rows = src.shape[0] // 2
            for part in range(2):
                here, sem = pl.ds(part * rows, rows), sems.at[2 * i + part]
                steps.append((
                    pltpu.make_async_copy(src.at[here], held.at[here], sem),
                    pltpu.make_async_copy(held.at[here], dst.at[here], sem),
                ))
                steps[-1][0].start()
        for come, leave in steps:
            come.wait()
            leave.start()
        for _, leave in steps:
            leave.wait()

    return pl.pallas_call(
        hand_over,
        out_shape=tuple(jax.ShapeDtypeStruct(r.shape, r.dtype) for r in results),
        in_specs=[anywhere] * 3,
        out_specs=[anywhere] * 3,
        scratch_shapes=[*(pltpu.VMEM(r.shape, r.dtype) for r in results), dma((6,))],
        cost_estimate=pl.CostEstimate(flops=0, bytes_accessed=5242880, transcendentals=0),
    )(*results)


def solution(mesh):
    in_specs = (P("row", "col"), P("row", "col"), P("row", "col"), P("col", "row"), P("col", "row"))
    out_specs = (P("row", "col"), P("col", "row"), P("col", "row"))
    return jax.shard_map(
        per_device, mesh=mesh, in_specs=in_specs, out_specs=out_specs, check_vma=False
    )
```

```python
import functools

import jax
import jax.numpy as jnp
from jax import lax
from jax.experimental import pallas as pl
from jax.experimental.pallas import tpu as pltpu
from jax.sharding import PartitionSpec as P

MESH = pl.DeviceIdType.MESH
BF = jnp.bfloat16
F32 = jnp.float32
NJ = 4
NK = 2
NP = 2
KC = 1024 // NK
NG = 4


def wrap(v):
    return lax.rem(v + 8, 4)


def block(i, n):
    return pl.ds(pl.multiple_of(i * n, n), n)


def kernel(
    g_ref, l_ref, r_ref, fm_ref, sm_ref,
    u_ref, fn_ref, sn_ref,
    gz, lh, rr, lp, lq, lr, rp, rot, dx, ep, eq, ee, up, u_out, fm, sm,
    l_comb, l_fin, r_comb, r_fin, e_comb, e_fin, u_comb, u_fin,
    ring_s, ring_r, sib_r, turn_s, turn_r, cast_s, cast_r, near,
):
    row, col = lax.axis_index("row"), lax.axis_index("col")
    y, c, x, z = row // 2, lax.rem(row, 2), col // 4, lax.rem(col, 4)
    other = 1 - c

    def dev(x, y, z, c):
        return (y * 2 + c, x * 4 + z)

    sib = dev(x, y, z, other)
    ring = {
        "x": (x, dev(wrap(x + 1), y, z, c), dev(wrap(x - 1), y, z, c)),
        "y": (y, dev(x, wrap(y + 1), z, c), dev(x, wrap(y - 1), z, c)),
        "z": (z, dev(x, y, wrap(z + 1), c), dev(x, y, wrap(z - 1), c)),
    }

    barrier = pltpu.get_barrier_semaphore()
    partners = [*ring["x"][1:], *ring["y"][1:], *ring["z"][1:], dev(x, y, wrap(z + 2), c), sib]
    for partner in partners:
        pl.semaphore_signal(barrier, inc=1, device_id=partner, device_id_type=MESH)

    @pl.when(x != y)
    def _():
        for cc in range(2):
            pl.semaphore_signal(barrier, inc=1, device_id=dev(y, x, z, cc), device_id_type=MESH)

    pl.semaphore_wait(barrier, jnp.where(x != y, len(partners) + 2, len(partners)))

    def remote(src, dst, ssem, rsem, device):
        return pltpu.make_async_remote_copy(
            src_ref=src, dst_ref=dst, send_sem=ssem, recv_sem=rsem, device_id=device, device_id_type=MESH
        )

    def arrived(dst, rsem):
        remote(dst, dst, ring_s.at[0], rsem, sib).wait_recv()

    def local(src, dst, n):
        copy = pltpu.make_async_copy(src, dst, near.at[n])
        copy.start()
        return copy

    class Ring:
        count = 0
        sems = 0

        def __init__(self, axis, chunks, two, four):
            self.pos, self.right_dev, self.left_dev = ring[axis]
            self.right, self.left, self.opp = wrap(self.pos + 1), wrap(self.pos - 1), wrap(self.pos + 2)
            self.op, self.base, self.two, self.four = Ring.count, Ring.sems, two, four
            Ring.count += 1
            Ring.sems += 2 * chunks

        def rsem(self, j, n):
            return ring_r.at[self.base + 2 * j + (n not in (0, 3))]

        def go(self, j, n, src, dst):
            remote(src, dst, ring_s.at[self.op], self.rsem(j, n), self.right_dev if n < 3 else self.left_dev).start()

        def wait_two(self, j):
            arrived(self.two, self.rsem(j, 0))

        def wait_four(self, j):
            arrived(self.four, self.rsem(j, 1))

    class Gather(Ring):
        def __init__(self, axis, chunks, two, four, src, dst):
            super().__init__(axis, chunks, two, four)
            self.src, self.dst = src, dst

        def start(self, j):
            self.go(j, 0, self.src(j, 0), self.dst(self.pos, j, 0))
            self.go(j, 3, self.src(j, 1), self.dst(self.pos, j, 1))
            self.go(j, 1, self.src(j, 1), self.dst(self.pos, j, 1))
            self.go(j, 4, self.src(j, 0), self.dst(self.pos, j, 0))

        def mid(self, j):
            self.wait_two(j)
            self.go(j, 2, self.dst(self.left, j, 0), self.dst(self.left, j, 0))
            self.go(j, 5, self.dst(self.right, j, 1), self.dst(self.right, j, 1))

        def end(self, j):
            self.wait_four(j)

    class Scatter(Ring):
        def __init__(self, axis, chunks, two, four, piece, comb, fin, out):
            super().__init__(axis, chunks, two, four)
            self.piece, self.comb, self.fin, self.out = piece, comb, fin, out

        def start(self, j):
            self.go(j, 0, self.piece(self.opp, j, 0), self.comb.at[j, 0])
            self.go(j, 3, self.piece(self.opp, j, 1), self.comb.at[j, 1])
            self.go(j, 1, self.piece(self.right, j, 1), self.fin.at[j, 0, 1])
            self.go(j, 4, self.piece(self.left, j, 0), self.fin.at[j, 1, 0])

        def mid(self, j):
            self.wait_two(j)
            for n, side, h in ((0, self.right, 0), (3, self.left, 1)):
                ref = self.piece(side, j, h)
                ref[...] = (ref[...].astype(F32) + self.comb[j, h].astype(F32)).astype(BF)
                self.go(j, n + 2, ref, self.fin.at[j, h, h])

        def end(self, j):
            self.wait_four(j)
            for h in range(2):
                total = self.piece(self.pos, j, h)[...].astype(F32)
                total = total + self.fin[j, 0, h].astype(F32) + self.fin[j, 1, h].astype(F32)
                self.out(j, h)[...] = total.astype(BF)

    def half_columns(ref, width=256):
        return lambda t, j, h: ref.at[j, pl.ds(2 * h, 2), c, :, block(t, width)]

    def half_pieces(ref):
        return lambda t, j, h: ref.at[j, t, pl.ds(2 * h, 2), c]

    small = lp.at[0, 0, 0], lp.at[0, 0, pl.ds(0, 2)]
    middle = lp.at[0, 0, pl.ds(0, 2)], lp.at[0, 0]
    large = lp.at[0, 0], lp.at[0, pl.ds(0, 2)]
    gh, kh = 1024 // NG // 2, KC // 2
    g_ag = Gather(
        "z", NG, *middle,
        lambda j, h: g_ref.at[pl.ds((2 * j + h) * gh, gh)],
        lambda t, j, h: gz.at[pl.ds((2 * j + h) * gh, gh), block(t, 256)],
    )
    l_ag = Gather(
        "x", NJ, *large,
        lambda j, h: l_ref.at[pl.ds(h * 512, 512), pl.ds(j * 128, 128)],
        lambda t, j, h: lh.at[j, pl.ds(h * 512, 512), block(t, 128)],
    )
    lr_rs = Scatter("y", NJ, *middle, half_pieces(lp), l_comb, l_fin, lambda j, h: half_columns(lr)(y, j, h))
    lr_ag = Gather("y", NJ, *middle, lambda j, h: half_columns(lr)(y, j, h), half_columns(lr))
    rot_rs = Scatter(
        "x", NJ, *middle, lambda t, j, h: rp.at[j, t, h], r_comb, r_fin,
        lambda j, h: rot.at[pl.ds(j * 128 + h * 64, 64)],
    )
    d_ag = Gather("x", NJ, *middle, lambda j, h: dx.at[j, x, h], lambda t, j, h: dx.at[j, t, h])
    e_half = half_columns(ee, 128)
    e_rs = Scatter("y", NP * NJ, *small, half_pieces(ep), e_comb, e_fin, lambda j, h: e_half(y, j, h))
    e_ag = Gather("y", NP * NJ, *small, lambda j, h: e_half(y, j, h), e_half)
    u_rs = Scatter(
        "z", NP * NK, *middle, lambda t, j, h: up.at[j // NK, t, pl.ds(j % NK * KC + h * kh, kh)], u_comb, u_fin,
        lambda j, h: u_out.at[pl.ds(j % NK * KC + h * kh, kh), pl.ds(j // NK * 128, 128)],
    )

    class Total:
        def __init__(self, rs, ag, parts, theirs, full, width, first, count):
            self.rs, self.ag, self.parts, self.theirs, self.full = rs, ag, parts, theirs, full
            self.width, self.first, self.count = width, first, count
            self.ssem = ring_s.at[Ring.count + (first > 0)]

        def swap(self, j):
            remote(
                self.parts.at[j, :, :, other], self.theirs.at[j], self.ssem, sib_r.at[self.first + j], sib
            ).start()

        def add(self, j):
            arrived(self.theirs.at[j], sib_r.at[self.first + j])
            for t in range(4):
                mine = self.parts[j, t, :, c].astype(F32)
                self.parts[j, t, :, c] = (mine + self.theirs[j, t].astype(F32)).astype(BF)
            self.rs.start(j)

        def share(self, j, t):
            ref = self.full.at[j, :, c, :, block(t, self.width)]
            remote(ref, ref, self.ssem, sib_r.at[self.first + self.count + j], sib).start()

        def turn(self, j):
            self.rs.end(j)
            self.ag.start(j)
            self.share(j, y)

        def end(self, j):
            self.ag.end(j)
            for t in (self.ag.left, self.ag.right, self.ag.opp):
                self.share(j, t)

        def ready(self, j):
            arrived(self.full.at[j, :, other], sib_r.at[self.first + self.count + j])

    lr_sum = Total(lr_rs, lr_ag, lp, lq, lr, 256, 0, NJ)
    e_sum = Total(e_rs, e_ag, ep, eq, ee, 128, 2 * NJ, NP * NJ)

    root = z // 2 == c
    keep = jnp.logical_and(x == y, root)
    cols_here = block(lax.rem(z, 2), 256)
    turned = remote(r_ref, rr.at[pl.ds(2 * c, 2), :, :, cols_here], turn_s.at[0], turn_r.at[c], dev(y, x, z, z // 2))
    casts = [
        remote(rr.at[:, :, :, cols_here], rr.at[:, :, :, cols_here], cast_s.at[d - 1], cast_r.at[lax.rem(z, 2)], dev(x, y, wrap(z + d), c))
        for d in (1, 2, 3)
    ]

    def right_send():
        @pl.when(jnp.logical_not(keep))
        def _():
            turned.start()

        @pl.when(keep)
        def _():
            pltpu.make_async_copy(r_ref, rr.at[pl.ds(2 * c, 2), :, :, cols_here], near.at[0]).start()

    def right_cast():
        @pl.when(root)
        def _():
            for cc in range(2):
                here = jnp.logical_and(x == y, c == cc)

                @pl.when(here)
                def _():
                    pltpu.make_async_copy(r_ref, rr.at[pl.ds(cc * 2, 2), :, :, cols_here], near.at[0]).wait()

                @pl.when(jnp.logical_not(here))
                def _():
                    arrived(rr.at[pl.ds(cc * 2, 2), :, :, cols_here], turn_r.at[cc])

            for cast in casts:
                cast.start()

    def right_ready():
        for s in range(2):
            @pl.when(2 * c + s != z)
            def _():
                arrived(rr.at[:, :, :, pl.ds(s * 256, 256)], cast_r.at[s])

    def left_product(j):
        part = lax.dot_general(lh[j], gz[...], (((0,), (0,)), ((), ())), preferred_element_type=F32).astype(BF)
        for t in range(4):
            lp[j, t] = part[:, t * 256 : t * 256 + 256].reshape(4, 2, 64, 256)
        lr_sum.swap(j)

    def right_product(j):
        lr_sum.ready(j)
        rp[j] = jnp.dot(
            lr[j].reshape(512, 1024), rr[...].reshape(1024, 512), preferred_element_type=F32
        ).astype(BF).reshape(4, 2, 64, 512)
        rot_rs.start(j)

    outs = []

    def moment_step(j):
        rot_rs.end(j)
        for h in range(2):
            rows = pl.ds(j * 128 + h * 64, 64)
            rotated = rot[rows].astype(F32)
            first_new = 0.9 * fm[rows] + 0.1 * rotated
            second_new = 0.95 * sm[rows] + 0.05 * rotated * rotated
            fm[rows] = first_new
            sm[rows] = second_new
            dx[j, x, h] = (first_new / (jnp.sqrt(second_new) + 1e-08)).astype(BF)
        d_ag.start(j)

    def right_back(p, j):
        if j not in waited:
            waited.append(j)
            d_ag.end(j)
        part = lax.dot_general(
            dx[j].reshape(512, 512), rr[:, p].reshape(512, 512), (((1,), (1,)), ((), ())), preferred_element_type=F32
        ).astype(BF)
        for t in range(4):
            ep[p * NJ + j, t] = part[:, t * 128 : t * 128 + 128].reshape(4, 2, 64, 128)
        e_sum.swap(p * NJ + j)

    def left_back(p, k):
        rows = pl.ds(k * KC, KC)
        total = jnp.dot(lh[0, rows], ee[p * NJ].reshape(512, 512), preferred_element_type=F32)
        for j in range(1, NJ):
            total = total + jnp.dot(lh[j, rows], ee[p * NJ + j].reshape(512, 512), preferred_element_type=F32)
        for t in range(4):
            up[p, t, rows] = total[:, t * 128 : t * 128 + 128].astype(BF)
        u_rs.start(p * NK + k)

    def last(j):
        u_rs.end(j)
        here = (pl.ds(j % NK * KC, KC), pl.ds(j // NK * 128, 128))
        outs.append(local(u_out.at[here], u_ref.at[here], 4 + j))

    waited = []
    l_ag.start(0)
    g_ag.start(0)
    own = [local(g_ref, gz.at[:, block(z, 256)], 1)]
    for j in range(4):
        own.append(local(l_ref.at[:, pl.ds(j * 128, 128)], lh.at[j, :, block(x, 128)], 4 + j))
    moments = [local(fm_ref, fm, 2), local(sm_ref, sm, 3)]
    l_ag.start(1)
    g_ag.start(1)
    g_ag.start(2)
    g_ag.start(3)
    g_ag.mid(0)
    l_ag.mid(0)
    g_ag.mid(1)
    g_ag.mid(2)
    l_ag.mid(1)
    g_ag.mid(3)
    right_send()
    l_ag.start(2)
    l_ag.start(3)
    for copy in own:
        copy.wait()
    l_ag.end(0)
    g_ag.end(0)
    g_ag.end(1)
    g_ag.end(2)
    g_ag.end(3)
    left_product(0)
    lr_sum.add(0)
    l_ag.end(1)
    left_product(1)
    lr_rs.mid(0)
    right_cast()
    lr_sum.add(1)
    lr_rs.mid(1)
    lr_sum.turn(0)
    l_ag.mid(3)
    lr_ag.mid(0)
    lr_sum.turn(1)
    l_ag.mid(2)
    lr_sum.end(0)
    l_ag.end(3)
    left_product(3)
    lr_ag.mid(1)
    right_ready()
    right_product(0)
    l_ag.end(2)
    left_product(2)
    lr_sum.add(3)
    lr_sum.end(1)
    rot_rs.mid(0)
    lr_sum.add(2)
    right_product(1)
    lr_rs.mid(3)
    for copy in moments:
        copy.wait()
    moment_step(0)
    lr_rs.mid(2)
    rot_rs.mid(1)
    lr_sum.turn(3)
    lr_ag.mid(3)
    moment_step(1)
    lr_sum.turn(2)
    d_ag.mid(0)
    d_ag.mid(1)
    lr_sum.end(3)
    lr_ag.mid(2)
    right_product(3)
    right_back(0, 0)
    right_back(0, 1)
    lr_sum.end(2)
    right_back(1, 1)
    e_sum.add(0)
    e_sum.add(1)
    rot_rs.mid(3)
    right_product(2)
    e_rs.mid(0)
    e_sum.add(5)
    right_back(1, 0)
    e_rs.mid(1)
    moment_step(3)
    e_sum.add(4)
    e_sum.turn(0)
    rot_rs.mid(2)
    e_rs.mid(5)
    e_sum.turn(1)
    e_rs.mid(4)
    d_ag.mid(3)
    e_ag.mid(0)
    moment_step(2)
    outs += [local(fm, fn_ref, 2), local(sm, sn_ref, 3)]
    e_sum.turn(5)
    e_ag.mid(1)
    right_back(0, 3)
    e_sum.turn(4)
    right_back(1, 3)
    e_sum.end(0)
    e_sum.add(3)
    e_ag.mid(5)
    d_ag.mid(2)
    e_sum.add(7)
    e_sum.end(1)
    e_ag.mid(4)
    e_rs.mid(3)
    right_back(0, 2)
    right_back(1, 2)
    e_sum.end(5)
    e_rs.mid(7)
    e_sum.add(2)
    e_sum.turn(3)
    e_rs.mid(2)
    e_sum.add(6)
    e_ag.mid(3)
    e_sum.turn(2)
    e_rs.mid(6)
    e_ag.mid(2)
    e_sum.end(3)
    e_sum.turn(7)
    e_sum.end(4)
    e_sum.turn(6)
    e_sum.end(2)
    for j in range(0, 4):
        e_sum.ready(j)
    left_back(0, 1)
    e_ag.mid(6)
    e_ag.mid(7)
    left_back(0, 0)
    e_sum.end(6)
    u_rs.mid(1)
    e_sum.end(7)
    for j in range(4, 8):
        e_sum.ready(j)
    left_back(1, 0)
    u_rs.mid(0)
    left_back(1, 1)
    u_rs.mid(2)
    u_rs.mid(3)
    last(0)
    last(1)
    last(2)
    last(3)
    for copy in outs:
        copy.wait()

    for op in range(Ring.count):
        whole = lp.at[pl.ds(0, 3)] if op == l_ag.op else lp.at[pl.ds(0, 3), pl.ds(0, 2)]
        remote(whole, whole, ring_s.at[op], ring_r.at[0], sib).wait_send()
    for total in (lr_sum, e_sum):
        remote(lh, lh, total.ssem, ring_r.at[0], sib).wait_send()

    @pl.when(jnp.logical_not(keep))
    def _():
        turned.wait_send()

    @pl.when(root)
    def _():
        for cast in casts:
            cast.wait_send()


def per_device(grad, basis_left, basis_right, first_moment, second_moment):
    dma = pltpu.SemaphoreType.DMA

    def scatter_buffers(chunks, half):
        return [pltpu.VMEM((chunks, 2, *half), BF), pltpu.VMEM((chunks, 2, 2, *half), BF)]

    scratch = [
        pltpu.VMEM((1024, 1024), BF),
        pltpu.VMEM((NJ, 1024, 512), BF),
        pltpu.VMEM((4, 2, 128, 512), BF),
        pltpu.VMEM((NJ, 4, 4, 2, 64, 256), BF),
        pltpu.VMEM((NJ, 4, 4, 64, 256), BF),
        pltpu.VMEM((NJ, 4, 2, 64, 1024), BF),
        pltpu.VMEM((NJ, 4, 2, 64, 512), BF),
        pltpu.VMEM((512, 512), BF),
        pltpu.VMEM((NJ, 4, 2, 64, 512), BF),
        pltpu.VMEM((NP * NJ, 4, 4, 2, 64, 128), BF),
        pltpu.VMEM((NP * NJ, 4, 4, 64, 128), BF),
        pltpu.VMEM((NP * NJ, 4, 2, 64, 512), BF),
        pltpu.VMEM((NP, 4, 1024, 128), BF),
        pltpu.VMEM((1024, 256), BF),
        pltpu.VMEM((512, 512), F32),
        pltpu.VMEM((512, 512), F32),
    ]
    for chunks, half in ((NJ, (2, 64, 256)), (NJ, (64, 512)), (NP * NJ, (2, 64, 128)), (NP * NK, (KC // 2, 128))):
        scratch += scatter_buffers(chunks, half)
    scratch += [dma((n,)) for n in (11, 2 * (NG + 5 * NJ + 2 * NP * NJ + NP * NK), 2 * (1 + NP) * NJ, 1, 2, 3, 2, 8)]
    anywhere = pl.BlockSpec(memory_space=pl.ANY)
    results = pl.pallas_call(
        kernel,
        out_shape=(
            jax.ShapeDtypeStruct((1024, 256), BF),
            jax.ShapeDtypeStruct((512, 512), F32),
            jax.ShapeDtypeStruct((512, 512), F32),
        ),
        in_specs=[anywhere] * 5,
        out_specs=[anywhere] * 3,
        scratch_shapes=scratch,
        compiler_params=pltpu.CompilerParams(
            collective_id=0, has_side_effects=True, vmem_limit_bytes=60 * 1024 * 1024
        ),
        cost_estimate=pl.CostEstimate(flops=12884901888, bytes_accessed=6553600, transcendentals=262144),
    )(grad, basis_left, basis_right.reshape(2, 2, 128, 256), first_moment, second_moment)

    def hand_over(u, fn, sn, u_out, fn_out, sn_out, u_held, fn_held, sn_held, sems):
        steps = []
        for i, (src, held, dst) in enumerate(((u, u_held, u_out), (fn, fn_held, fn_out), (sn, sn_held, sn_out))):
            rows = src.shape[0] // 2
            for part in range(2):
                here, sem = pl.ds(part * rows, rows), sems.at[2 * i + part]
                steps.append((
                    pltpu.make_async_copy(src.at[here], held.at[here], sem),
                    pltpu.make_async_copy(held.at[here], dst.at[here], sem),
                ))
                steps[-1][0].start()
        for come, leave in steps:
            come.wait()
            leave.start()
        for _, leave in steps:
            leave.wait()

    return pl.pallas_call(
        hand_over,
        out_shape=tuple(jax.ShapeDtypeStruct(r.shape, r.dtype) for r in results),
        in_specs=[anywhere] * 3,
        out_specs=[anywhere] * 3,
        scratch_shapes=[*(pltpu.VMEM(r.shape, r.dtype) for r in results), dma((6,))],
        cost_estimate=pl.CostEstimate(flops=0, bytes_accessed=5242880, transcendentals=0),
    )(*results)


def solution(mesh):
    in_specs = (P("row", "col"), P("row", "col"), P("row", "col"), P("col", "row"), P("col", "row"))
    out_specs = (P("row", "col"), P("col", "row"), P("col", "row"))
    return jax.shard_map(
        per_device, mesh=mesh, in_specs=in_specs, out_specs=out_specs, check_vma=False
    )
```

```python
import functools

import jax
import jax.numpy as jnp
from jax import lax
from jax.experimental import pallas as pl
from jax.experimental.pallas import tpu as pltpu
from jax.sharding import PartitionSpec as P

MESH = pl.DeviceIdType.MESH
BF = jnp.bfloat16
F32 = jnp.float32
NJ = 4
NK = 2
NP = 2
KC = 1024 // NK
NG = 4


def wrap(v):
    return lax.rem(v + 8, 4)


def block(i, n):
    return pl.ds(pl.multiple_of(i * n, n), n)


def kernel(
    g_ref, l_ref, r_ref, fm_ref, sm_ref,
    u_ref, fn_ref, sn_ref,
    gz, lh, rr, lp, lq, lr, rp, rot, dx, ep, eq, ee, up, u_out, fm, sm,
    l_comb, l_fin, r_comb, r_fin, e_comb, e_fin, u_comb, u_fin,
    ring_s, ring_r, sib_r, turn_s, turn_r, cast_s, cast_r, near,
):
    row, col = lax.axis_index("row"), lax.axis_index("col")
    y, c, x, z = row // 2, lax.rem(row, 2), col // 4, lax.rem(col, 4)
    other = 1 - c

    def dev(x, y, z, c):
        return (y * 2 + c, x * 4 + z)

    sib = dev(x, y, z, other)
    ring = {
        "x": (x, dev(wrap(x + 1), y, z, c), dev(wrap(x - 1), y, z, c)),
        "y": (y, dev(x, wrap(y + 1), z, c), dev(x, wrap(y - 1), z, c)),
        "z": (z, dev(x, y, wrap(z + 1), c), dev(x, y, wrap(z - 1), c)),
    }

    barrier = pltpu.get_barrier_semaphore()
    partners = [*ring["x"][1:], *ring["y"][1:], *ring["z"][1:], dev(x, y, wrap(z + 2), c), sib]
    for partner in partners:
        pl.semaphore_signal(barrier, inc=1, device_id=partner, device_id_type=MESH)

    @pl.when(x != y)
    def _():
        for cc in range(2):
            pl.semaphore_signal(barrier, inc=1, device_id=dev(y, x, z, cc), device_id_type=MESH)

    pl.semaphore_wait(barrier, jnp.where(x != y, len(partners) + 2, len(partners)))

    def remote(src, dst, ssem, rsem, device):
        return pltpu.make_async_remote_copy(
            src_ref=src, dst_ref=dst, send_sem=ssem, recv_sem=rsem, device_id=device, device_id_type=MESH
        )

    def arrived(dst, rsem):
        remote(dst, dst, ring_s.at[0], rsem, sib).wait_recv()

    def local(src, dst, n):
        copy = pltpu.make_async_copy(src, dst, near.at[n])
        copy.start()
        return copy

    class Ring:
        count = 0
        sems = 0

        def __init__(self, axis, chunks, two, four):
            self.pos, self.right_dev, self.left_dev = ring[axis]
            self.right, self.left, self.opp = wrap(self.pos + 1), wrap(self.pos - 1), wrap(self.pos + 2)
            self.op, self.base, self.two, self.four = Ring.count, Ring.sems, two, four
            Ring.count += 1
            Ring.sems += 2 * chunks

        def rsem(self, j, n):
            return ring_r.at[self.base + 2 * j + (n not in (0, 3))]

        def go(self, j, n, src, dst):
            remote(src, dst, ring_s.at[self.op], self.rsem(j, n), self.right_dev if n < 3 else self.left_dev).start()

        def wait_two(self, j):
            arrived(self.two, self.rsem(j, 0))

        def wait_four(self, j):
            arrived(self.four, self.rsem(j, 1))

    class Gather(Ring):
        def __init__(self, axis, chunks, two, four, src, dst):
            super().__init__(axis, chunks, two, four)
            self.src, self.dst = src, dst

        def start(self, j):
            self.go(j, 0, self.src(j, 0), self.dst(self.pos, j, 0))
            self.go(j, 3, self.src(j, 1), self.dst(self.pos, j, 1))
            self.go(j, 1, self.src(j, 1), self.dst(self.pos, j, 1))
            self.go(j, 4, self.src(j, 0), self.dst(self.pos, j, 0))

        def mid(self, j):
            self.wait_two(j)
            self.go(j, 2, self.dst(self.left, j, 0), self.dst(self.left, j, 0))
            self.go(j, 5, self.dst(self.right, j, 1), self.dst(self.right, j, 1))

        def end(self, j):
            self.wait_four(j)

    class Scatter(Ring):
        def __init__(self, axis, chunks, two, four, piece, comb, fin, out):
            super().__init__(axis, chunks, two, four)
            self.piece, self.comb, self.fin, self.out = piece, comb, fin, out

        def start(self, j):
            self.go(j, 0, self.piece(self.opp, j, 0), self.comb.at[j, 0])
            self.go(j, 3, self.piece(self.opp, j, 1), self.comb.at[j, 1])
            self.go(j, 1, self.piece(self.right, j, 1), self.fin.at[j, 0, 1])
            self.go(j, 4, self.piece(self.left, j, 0), self.fin.at[j, 1, 0])

        def mid(self, j):
            self.wait_two(j)
            for n, side, h in ((0, self.right, 0), (3, self.left, 1)):
                ref = self.piece(side, j, h)
                ref[...] = (ref[...].astype(F32) + self.comb[j, h].astype(F32)).astype(BF)
                self.go(j, n + 2, ref, self.fin.at[j, h, h])

        def end(self, j):
            self.wait_four(j)
            for h in range(2):
                total = self.piece(self.pos, j, h)[...].astype(F32)
                total = total + self.fin[j, 0, h].astype(F32) + self.fin[j, 1, h].astype(F32)
                self.out(j, h)[...] = total.astype(BF)

    def half_columns(ref, width=256):
        return lambda t, j, h: ref.at[j, pl.ds(2 * h, 2), c, :, block(t, width)]

    def half_pieces(ref):
        return lambda t, j, h: ref.at[j, t, pl.ds(2 * h, 2), c]

    small = lp.at[0, 0, 0], lp.at[0, 0, pl.ds(0, 2)]
    middle = lp.at[0, 0, pl.ds(0, 2)], lp.at[0, 0]
    large = lp.at[0, 0], lp.at[0, pl.ds(0, 2)]
    gh, kh = 1024 // NG // 2, KC // 2
    g_ag = Gather(
        "z", NG, *middle,
        lambda j, h: g_ref.at[pl.ds((2 * j + h) * gh, gh)],
        lambda t, j, h: gz.at[pl.ds((2 * j + h) * gh, gh), block(t, 256)],
    )
    l_ag = Gather(
        "x", NJ, *large,
        lambda j, h: l_ref.at[pl.ds(h * 512, 512), pl.ds(j * 128, 128)],
        lambda t, j, h: lh.at[j, pl.ds(h * 512, 512), block(t, 128)],
    )
    lr_rs = Scatter("y", NJ, *middle, half_pieces(lp), l_comb, l_fin, lambda j, h: half_columns(lr)(y, j, h))
    lr_ag = Gather("y", NJ, *middle, lambda j, h: half_columns(lr)(y, j, h), half_columns(lr))
    rot_rs = Scatter(
        "x", NJ, *middle, lambda t, j, h: rp.at[j, t, h], r_comb, r_fin,
        lambda j, h: rot.at[pl.ds(j * 128 + h * 64, 64)],
    )
    d_ag = Gather("x", NJ, *middle, lambda j, h: dx.at[j, x, h], lambda t, j, h: dx.at[j, t, h])
    e_half = half_columns(ee, 128)
    e_rs = Scatter("y", NP * NJ, *small, half_pieces(ep), e_comb, e_fin, lambda j, h: e_half(y, j, h))
    e_ag = Gather("y", NP * NJ, *small, lambda j, h: e_half(y, j, h), e_half)
    u_rs = Scatter(
        "z", NP * NK, *middle, lambda t, j, h: up.at[j // NK, t, pl.ds(j % NK * KC + h * kh, kh)], u_comb, u_fin,
        lambda j, h: u_out.at[pl.ds(j % NK * KC + h * kh, kh), pl.ds(j // NK * 128, 128)],
    )

    class Total:
        def __init__(self, rs, ag, parts, theirs, full, width, first, count):
            self.rs, self.ag, self.parts, self.theirs, self.full = rs, ag, parts, theirs, full
            self.width, self.first, self.count = width, first, count
            self.ssem = ring_s.at[Ring.count + (first > 0)]

        def swap(self, j):
            remote(
                self.parts.at[j, :, :, other], self.theirs.at[j], self.ssem, sib_r.at[self.first + j], sib
            ).start()

        def add(self, j):
            arrived(self.theirs.at[j], sib_r.at[self.first + j])
            for t in range(4):
                mine = self.parts[j, t, :, c].astype(F32)
                self.parts[j, t, :, c] = (mine + self.theirs[j, t].astype(F32)).astype(BF)
            self.rs.start(j)

        def share(self, j, t):
            ref = self.full.at[j, :, c, :, block(t, self.width)]
            remote(ref, ref, self.ssem, sib_r.at[self.first + self.count + j], sib).start()

        def turn(self, j):
            self.rs.end(j)
            self.ag.start(j)
            self.share(j, y)

        def end(self, j):
            self.ag.end(j)
            for t in (self.ag.left, self.ag.right, self.ag.opp):
                self.share(j, t)

        def ready(self, j):
            arrived(self.full.at[j, :, other], sib_r.at[self.first + self.count + j])

    lr_sum = Total(lr_rs, lr_ag, lp, lq, lr, 256, 0, NJ)
    e_sum = Total(e_rs, e_ag, ep, eq, ee, 128, 2 * NJ, NP * NJ)

    root = z // 2 == c
    keep = jnp.logical_and(x == y, root)
    cols_here = block(lax.rem(z, 2), 256)
    turned = remote(r_ref, rr.at[pl.ds(2 * c, 2), :, :, cols_here], turn_s.at[0], turn_r.at[c], dev(y, x, z, z // 2))
    casts = [
        remote(rr.at[:, :, :, cols_here], rr.at[:, :, :, cols_here], cast_s.at[d - 1], cast_r.at[lax.rem(z, 2)], dev(x, y, wrap(z + d), c))
        for d in (1, 2, 3)
    ]

    def right_send():
        @pl.when(jnp.logical_not(keep))
        def _():
            turned.start()

        @pl.when(keep)
        def _():
            pltpu.make_async_copy(r_ref, rr.at[pl.ds(2 * c, 2), :, :, cols_here], near.at[0]).start()

    def right_cast():
        @pl.when(root)
        def _():
            for cc in range(2):
                here = jnp.logical_and(x == y, c == cc)

                @pl.when(here)
                def _():
                    pltpu.make_async_copy(r_ref, rr.at[pl.ds(cc * 2, 2), :, :, cols_here], near.at[0]).wait()

                @pl.when(jnp.logical_not(here))
                def _():
                    arrived(rr.at[pl.ds(cc * 2, 2), :, :, cols_here], turn_r.at[cc])

            for cast in casts:
                cast.start()

    def right_ready():
        for s in range(2):
            @pl.when(2 * c + s != z)
            def _():
                arrived(rr.at[:, :, :, pl.ds(s * 256, 256)], cast_r.at[s])

    def left_product(j):
        part = lax.dot_general(lh[j], gz[...], (((0,), (0,)), ((), ())), preferred_element_type=F32).astype(BF)
        for t in range(4):
            lp[j, t] = part[:, t * 256 : t * 256 + 256].reshape(4, 2, 64, 256)
        lr_sum.swap(j)

    def right_product(j):
        lr_sum.ready(j)
        rp[j] = jnp.dot(
            lr[j].reshape(512, 1024), rr[...].reshape(1024, 512), preferred_element_type=F32
        ).astype(BF).reshape(4, 2, 64, 512)
        rot_rs.start(j)

    outs = []

    def moment_step(j):
        rot_rs.end(j)
        for h in range(2):
            rows = pl.ds(j * 128 + h * 64, 64)
            rotated = rot[rows].astype(F32)
            first_new = 0.9 * fm[rows] + 0.1 * rotated
            second_new = 0.95 * sm[rows] + 0.05 * rotated * rotated
            fm[rows] = first_new
            sm[rows] = second_new
            dx[j, x, h] = (first_new / (jnp.sqrt(second_new) + 1e-08)).astype(BF)
        d_ag.start(j)

    def right_back(p, j):
        if j not in waited:
            waited.append(j)
            d_ag.end(j)
        part = lax.dot_general(
            dx[j].reshape(512, 512), rr[:, p].reshape(512, 512), (((1,), (1,)), ((), ())), preferred_element_type=F32
        ).astype(BF)
        for t in range(4):
            ep[p * NJ + j, t] = part[:, t * 128 : t * 128 + 128].reshape(4, 2, 64, 128)
        e_sum.swap(p * NJ + j)

    def left_back(p, k):
        rows = pl.ds(k * KC, KC)
        total = jnp.dot(lh[0, rows], ee[p * NJ].reshape(512, 512), preferred_element_type=F32)
        for j in range(1, NJ):
            total = total + jnp.dot(lh[j, rows], ee[p * NJ + j].reshape(512, 512), preferred_element_type=F32)
        for t in range(4):
            up[p, t, rows] = total[:, t * 128 : t * 128 + 128].astype(BF)
        u_rs.start(p * NK + k)

    def last(j):
        u_rs.end(j)
        here = (pl.ds(j % NK * KC, KC), pl.ds(j // NK * 128, 128))
        outs.append(local(u_out.at[here], u_ref.at[here], 4 + j))

    waited = []
    l_ag.start(0)
    g_ag.start(0)
    own = [local(g_ref, gz.at[:, block(z, 256)], 1)]
    for j in range(4):
        own.append(local(l_ref.at[:, pl.ds(j * 128, 128)], lh.at[j, :, block(x, 128)], 4 + j))
    moments = [local(fm_ref, fm, 2), local(sm_ref, sm, 3)]
    g_ag.start(1)
    g_ag.start(2)
    l_ag.start(1)
    g_ag.mid(0)
    l_ag.mid(0)
    g_ag.mid(1)
    g_ag.mid(2)
    l_ag.mid(1)
    right_send()
    g_ag.start(3)
    l_ag.start(2)
    l_ag.start(3)
    g_ag.mid(3)
    for copy in own:
        copy.wait()
    l_ag.end(0)
    g_ag.end(0)
    g_ag.end(1)
    g_ag.end(2)
    g_ag.end(3)
    left_product(0)
    l_ag.end(1)
    left_product(1)
    lr_sum.add(0)
    lr_sum.add(1)
    right_cast()
    lr_rs.mid(0)
    l_ag.mid(2)
    lr_rs.mid(1)
    lr_sum.turn(0)
    l_ag.mid(3)
    lr_sum.turn(1)
    lr_ag.mid(0)
    lr_ag.mid(1)
    l_ag.end(2)
    left_product(2)
    lr_sum.end(0)
    lr_sum.end(1)
    lr_sum.add(2)
    right_ready()
    right_product(0)
    right_product(1)
    l_ag.end(3)
    left_product(3)
    lr_rs.mid(2)
    rot_rs.mid(0)
    lr_sum.add(3)
    lr_sum.turn(2)
    rot_rs.mid(1)
    lr_rs.mid(3)
    for copy in moments:
        copy.wait()
    moment_step(0)
    moment_step(1)
    lr_ag.mid(2)
    d_ag.mid(0)
    lr_sum.turn(3)
    lr_sum.end(2)
    d_ag.mid(1)
    right_product(2)
    lr_ag.mid(3)
    right_back(0, 0)
    right_back(0, 1)
    right_back(1, 1)
    e_sum.add(1)
    rot_rs.mid(2)
    lr_sum.end(3)
    right_product(3)
    e_rs.mid(1)
    e_sum.add(0)
    e_sum.add(5)
    moment_step(2)
    right_back(1, 0)
    e_sum.turn(1)
    e_sum.add(4)
    rot_rs.mid(3)
    e_rs.mid(0)
    e_rs.mid(5)
    e_ag.mid(1)
    d_ag.mid(2)
    e_rs.mid(4)
    moment_step(3)
    outs += [local(fm, fn_ref, 2), local(sm, sn_ref, 3)]
    e_sum.turn(0)
    e_sum.turn(5)
    right_back(0, 2)
    e_sum.turn(4)
    d_ag.mid(3)
    e_ag.mid(0)
    e_sum.add(2)
    e_ag.mid(5)
    right_back(1, 2)
    e_ag.mid(4)
    e_sum.add(6)
    e_sum.end(0)
    right_back(0, 3)
    e_sum.add(3)
    e_sum.end(5)
    e_sum.end(4)
    e_rs.mid(2)
    e_sum.end(1)
    e_rs.mid(6)
    right_back(1, 3)
    e_rs.mid(3)
    e_sum.add(7)
    e_sum.turn(2)
    e_sum.turn(3)
    e_ag.mid(2)
    e_rs.mid(7)
    e_ag.mid(3)
    e_sum.turn(6)
    e_sum.end(2)
    e_sum.turn(7)
    e_sum.end(3)
    e_ag.mid(6)
    for j in range(0, 4):
        e_sum.ready(j)
    left_back(0, 0)
    e_ag.mid(7)
    left_back(0, 1)
    e_sum.end(7)
    u_rs.mid(0)
    e_sum.end(6)
    for j in range(4, 8):
        e_sum.ready(j)
    left_back(1, 1)
    u_rs.mid(1)
    left_back(1, 0)
    last(0)
    u_rs.mid(3)
    last(1)
    u_rs.mid(2)
    last(3)
    last(2)
    for copy in outs:
        copy.wait()

    for op in range(Ring.count):
        whole = lp.at[pl.ds(0, 3)] if op == l_ag.op else lp.at[pl.ds(0, 3), pl.ds(0, 2)]
        remote(whole, whole, ring_s.at[op], ring_r.at[0], sib).wait_send()
    for total in (lr_sum, e_sum):
        remote(lh, lh, total.ssem, ring_r.at[0], sib).wait_send()

    @pl.when(jnp.logical_not(keep))
    def _():
        turned.wait_send()

    @pl.when(root)
    def _():
        for cast in casts:
            cast.wait_send()


def per_device(grad, basis_left, basis_right, first_moment, second_moment):
    dma = pltpu.SemaphoreType.DMA

    def scatter_buffers(chunks, half):
        return [pltpu.VMEM((chunks, 2, *half), BF), pltpu.VMEM((chunks, 2, 2, *half), BF)]

    scratch = [
        pltpu.VMEM((1024, 1024), BF),
        pltpu.VMEM((NJ, 1024, 512), BF),
        pltpu.VMEM((4, 2, 128, 512), BF),
        pltpu.VMEM((NJ, 4, 4, 2, 64, 256), BF),
        pltpu.VMEM((NJ, 4, 4, 64, 256), BF),
        pltpu.VMEM((NJ, 4, 2, 64, 1024), BF),
        pltpu.VMEM((NJ, 4, 2, 64, 512), BF),
        pltpu.VMEM((512, 512), BF),
        pltpu.VMEM((NJ, 4, 2, 64, 512), BF),
        pltpu.VMEM((NP * NJ, 4, 4, 2, 64, 128), BF),
        pltpu.VMEM((NP * NJ, 4, 4, 64, 128), BF),
        pltpu.VMEM((NP * NJ, 4, 2, 64, 512), BF),
        pltpu.VMEM((NP, 4, 1024, 128), BF),
        pltpu.VMEM((1024, 256), BF),
        pltpu.VMEM((512, 512), F32),
        pltpu.VMEM((512, 512), F32),
    ]
    for chunks, half in ((NJ, (2, 64, 256)), (NJ, (64, 512)), (NP * NJ, (2, 64, 128)), (NP * NK, (KC // 2, 128))):
        scratch += scatter_buffers(chunks, half)
    scratch += [dma((n,)) for n in (11, 2 * (NG + 5 * NJ + 2 * NP * NJ + NP * NK), 2 * (1 + NP) * NJ, 1, 2, 3, 2, 8)]
    anywhere = pl.BlockSpec(memory_space=pl.ANY)
    results = pl.pallas_call(
        kernel,
        out_shape=(
            jax.ShapeDtypeStruct((1024, 256), BF),
            jax.ShapeDtypeStruct((512, 512), F32),
            jax.ShapeDtypeStruct((512, 512), F32),
        ),
        in_specs=[anywhere] * 5,
        out_specs=[anywhere] * 3,
        scratch_shapes=scratch,
        compiler_params=pltpu.CompilerParams(
            collective_id=0, has_side_effects=True, vmem_limit_bytes=60 * 1024 * 1024
        ),
        cost_estimate=pl.CostEstimate(flops=12884901888, bytes_accessed=6553600, transcendentals=262144),
    )(grad, basis_left, basis_right.reshape(2, 2, 128, 256), first_moment, second_moment)

    def hand_over(u, fn, sn, u_out, fn_out, sn_out, u_held, fn_held, sn_held, sems):
        steps = []
        for i, (src, held, dst) in enumerate(((u, u_held, u_out), (fn, fn_held, fn_out), (sn, sn_held, sn_out))):
            rows = src.shape[0] // 2
            for part in range(2):
                here, sem = pl.ds(part * rows, rows), sems.at[2 * i + part]
                steps.append((
                    pltpu.make_async_copy(src.at[here], held.at[here], sem),
                    pltpu.make_async_copy(held.at[here], dst.at[here], sem),
                ))
                steps[-1][0].start()
        for come, leave in steps:
            come.wait()
            leave.start()
        for _, leave in steps:
            leave.wait()

    return pl.pallas_call(
        hand_over,
        out_shape=tuple(jax.ShapeDtypeStruct(r.shape, r.dtype) for r in results),
        in_specs=[anywhere] * 3,
        out_specs=[anywhere] * 3,
        scratch_shapes=[*(pltpu.VMEM(r.shape, r.dtype) for r in results), dma((6,))],
        cost_estimate=pl.CostEstimate(flops=0, bytes_accessed=5242880, transcendentals=0),
    )(*results)


def solution(mesh):
    in_specs = (P("row", "col"), P("row", "col"), P("row", "col"), P("col", "row"), P("col", "row"))
    out_specs = (P("row", "col"), P("col", "row"), P("col", "row"))
    return jax.shard_map(
        per_device, mesh=mesh, in_specs=in_specs, out_specs=out_specs, check_vma=False
    )
```
